512 devices in a mesh: slab: 64 (over z_hi, y, core), dp: 8 (over z_lo, x).
Axes of the slice: x: 4, y: 8, z: 8 (z_hi: 4, z_lo: 2; z = z_hi * 2 + z_lo), core: 2. Of those that a mesh axis runs over, the one named last changes fastest.
Arguments:
- universe: bfloat16 [8, 4, 256, 4, 512], P('dp', None, 'slab'), may hold values from -6 to 6
- cotangent: bfloat16 [8, 64, 64, 1, 128], P('dp', None, 'slab'), may hold values from -0.15625 to 0.15625
- conv1_weight: bfloat16 [32, 108], replicated, may hold values from -0.625 to 0.625
- conv1_bias: float32 [32], replicated, may hold values from -3 to 3
- conv2_weight: bfloat16 [64, 864], replicated, may hold values from -0.21875 to 0.21875
- conv2_bias: float32 [64], replicated, may hold values from -3 to 3
- owners: int32 [460, 1], replicated, may hold values from 0 to 7; in each aligned block of 460 rows (0 to 459, 460 to 919, ...) at most 138 rows name the same one
- accumulated: float32 [1104, 128], P('dp'), may hold values from -1 to 1
Outputs:
- features: bfloat16 [8, 64, 64, 1, 128], P('dp', None, 'slab')
- owned: float32 [1104, 128], P('dp')
The draws below stay inside these ranges and needn't reach their ends.
Inputs may be any that keep to these rules, and one draw needn't show every extreme that they name: `owners`: each index of dp owns at most 138 blocks, exactly 138 for one of them, and at least one for each.
All inputs are finite; a program needn't handle non-finite values.
Results may differ from the reference program's by a relative error of at most 0.0014.
The reference program's roundings to bfloat16 on the way (of `pooled`, `delta_two` and `delta_one`) count: a program that leaves them out, or rounds other values in their place, can miss the bound.
Values may be sent and summed in bfloat16 or wider, within the bound.
No kernel may reach another device: no remote copies, remote signals or barrier semaphores. Data moves between devices by JAX's collectives and lax.ppermute only.
A program may use at most 64 MiB of HBM per device.

```python
import math
import jax
import jax.numpy as jnp
import numpy as np
from jax import lax

CIN = 4
C1 = 32
C2 = 64
DZ = 4
HY = 4
HX = 512
UNIV = 8
DEPTH = 256
NB = 460
CAP = 138
N_SLAB = 64
N_DP = 8


def block_levels(own_key, shape, cuts, least, largest):
    def one(position, blocks):
        steps = jax.random.uniform(jax.random.fold_in(jax.random.fold_in(own_key, 6), position), (blocks,), jnp.float32, least / len(cuts), largest / len(cuts))
        return jnp.repeat(jnp.exp(steps), shape[position] // blocks).reshape((-1,) + (1,) * (len(shape) - position - 1))

    gain = one(*cuts[0])
    for cut in cuts[1:]:
        gain = gain * one(*cut)
    return gain


def routed_block(rng, own, number, rows, number_of, top, limit, skew):
    sequence = jax.random.permutation(rng, number_of)
    crowded, ordinary = portions_of(number_of, rows * top, limit, skew, True), portions_of(number_of, rows * top, limit, skew, False)
    places = jnp.arange(number_of)

    def named(tallies, offset_by):
        used = int((tallies > 0).sum())
        fixed = max(1, used // 4)
        moved = fixed + (places - fixed + offset_by * (used - fixed)) % max(1, number_of - fixed)
        return jnp.zeros((number_of,), jnp.int32).at[sequence[jnp.where(places < fixed, places, moved)]].set(jnp.asarray(tallies, jnp.int32))

    tallies = jnp.where(number % 4 == 0, named(crowded, number // 4), named(ordinary, number - number // 4 - 1))
    mixed = jax.random.permutation(jax.random.fold_in(own, 3), number_of)
    donor, taker = mixed[0:number_of // 2 * 2:2], mixed[1:number_of // 2 * 2:2]
    slack = jnp.minimum(tallies[donor] - 1, limit - tallies[taker]) // 2
    slack = jnp.where((donor == sequence[0]) | (taker == sequence[0]) | (tallies[taker] == 0), 0, jnp.maximum(slack, 0))
    moved = jax.random.randint(jax.random.fold_in(own, 4), (number_of // 2,), 0, 1 << 20) % (slack + 1)
    tallies = tallies.at[donor].add(-moved).at[taker].add(moved)
    labels = jnp.searchsorted(jnp.cumsum(tallies), jnp.arange(rows * top), side="right").astype(jnp.int32)
    grid = labels.reshape(top, rows).T
    grid = grid[jax.random.permutation(jax.random.fold_in(own, 1), rows)]
    offset_by = jax.random.randint(jax.random.fold_in(own, 2), (rows, 1), 0, top)
    return jnp.take_along_axis(grid, (jnp.arange(top)[None, :] + offset_by) % top, axis=1)


def portions_of(amount, total, bound, skew, full):
    loads = [(1 << 20) // math.isqrt(rank ** skew) + 1 for rank in range(1, amount + 1)]
    largest = bound if full else min(bound, max(-(-total // amount), total * loads[0] // sum(loads)))
    least = 1 if total - largest >= amount - 1 else 0
    given, rest = [largest] + [least] * (amount - 1), total - largest - least * (amount - 1)
    while rest > 0:
        free = [i for i in range(1, amount) if given[i] < largest] or [i for i in range(1, amount) if given[i] < bound]
        pool, budget = sum([loads[i] for i in free]), rest
        for i in free:
            addition = min(bound - given[i], max(1, budget * loads[i] // pool), rest)
            given[i] = given[i] + addition
            rest = rest - addition
    return np.array(given)


def centred(key, extent, deviation, most, cuts=(), held_as=jnp.bfloat16):
    values = deviation * jax.random.normal(key, extent, jnp.float32)
    if cuts:
        values = values * block_levels(key, extent, cuts, -0.22, 0.18)
    return jnp.clip(values, -most, most).astype(held_as)


def setup_inputs(seed: int = 0) -> dict:
    keys = jax.random.split(jax.random.key(seed), 9)
    universe = centred(keys[0], (UNIV, CIN, DEPTH, HY, HX), 1.0, 6.0, ((0, 8), (2, 64)))
    cotangent = centred(keys[1], (UNIV, C2, DEPTH // 4, HY // 4, HX // 4), (50 * (DZ * HY * HX * N_SLAB * N_DP) ** -0.5), 0.15625, ((0, 8), (2, 64)))
    conv1_weight = centred(keys[2], (C1, 27 * CIN), (27 * CIN) ** -0.5, 0.625)
    conv1_bias = centred(keys[3], (C1,), 0.5, 3.0, (), jnp.float32)
    conv2_weight = centred(keys[4], (C2, 27 * C1), (27 * C1) ** -0.5, 0.21875)
    conv2_bias = centred(keys[5], (C2,), 0.5, 3.0, (), jnp.float32)
    owners_keys = jax.random.split(jax.random.fold_in(keys[6], 1), NB // NB)
    owners_turns = jax.random.permutation(jax.random.fold_in(keys[6], 3), NB // NB)
    owners = jax.vmap(lambda own, number: routed_block(jax.random.fold_in(keys[6], 2), own, number, NB, N_DP, 1, CAP, 2))(owners_keys, owners_turns).reshape((NB, 1))
    accumulated = jnp.clip(jax.random.uniform(keys[7], (N_DP * CAP, 128), jnp.float32, -1.0, 1.0) * block_levels(keys[7], (N_DP * CAP, 128), ((0, 8),), -0.4, 0.0), -1.0, 1.0)
    return {"universe": universe, "cotangent": cotangent, "conv1_weight": conv1_weight, "conv1_bias": conv1_bias, "conv2_weight": conv2_weight, "conv2_bias": conv2_bias, "owners": owners, "accumulated": accumulated}


SLOPE = 0.3
OFFSETS = [(first, second, third) for first in range(3) for second in range(3) for third in range(3)]

def pad_field(field):
    wrapped = jnp.pad(field, ((0, 0), (1, 1), (0, 0), (0, 0)), mode='wrap')
    return jnp.pad(wrapped, ((0, 0), (0, 0), (1, 1), (1, 1)))

def shifted(padded, number, deep_rows, high_rows, wide_rows):
    first, second, third = OFFSETS[number]
    window = padded[:, first:first + deep_rows, second:second + high_rows, third:third + wide_rows]
    return window.reshape(padded.shape[0], deep_rows * high_rows * wide_rows)

def convolve(padded, weight, deep_rows, high_rows, wide_rows):
    kernel = weight.reshape(weight.shape[0], 27, padded.shape[0])
    running = jnp.zeros((weight.shape[0], deep_rows * high_rows * wide_rows), jnp.float32)
    for number in range(27):
        running = running + jnp.dot(kernel[:, number], shifted(padded, number, deep_rows, high_rows, wide_rows), preferred_element_type=jnp.float32)
    return running.reshape(weight.shape[0], deep_rows, high_rows, wide_rows)

def weight_grad(delta, padded, deep_rows, high_rows, wide_rows):
    pieces = [jnp.dot(delta, shifted(padded, number, deep_rows, high_rows, wide_rows).T, preferred_element_type=jnp.float32) for number in range(27)]
    return jnp.stack(pieces, axis=1).reshape(delta.shape[0], -1)

def input_grad(delta_padded, weight, chans_in, deep_rows, high_rows, wide_rows):
    kernel = weight.reshape(weight.shape[0], 27, chans_in)
    running = jnp.zeros((chans_in, deep_rows * high_rows * wide_rows), jnp.float32)
    for number in range(27):
        running = running + jnp.dot(kernel[:, number].T, shifted(delta_padded, 26 - number, deep_rows, high_rows, wide_rows), preferred_element_type=jnp.float32)
    return running.reshape(chans_in, deep_rows, high_rows, wide_rows)

def average(field):
    chans, deep_rows, high_rows, wide_rows = field.shape
    return field.reshape(chans, deep_rows // 2, 2, high_rows // 2, 2, wide_rows // 2, 2).mean(axis=(2, 4, 6))

def spread_back(field):
    return jnp.repeat(jnp.repeat(jnp.repeat(field, 2, axis=1), 2, axis=2), 2, axis=3) * 0.125

def leaky_relu(value):
    return jnp.where(value > 0, value, SLOPE * value)

def slope_mask(value):
    return jnp.where(value > 0, 1.0, SLOPE)

def place_blocks(owners, blocks, ranks, capacity):
    owner_of = owners[:, 0]
    member = (owner_of[:, None] == jnp.arange(ranks, dtype=jnp.int32)[None, :]).astype(jnp.int32)
    before = jnp.cumsum(member, axis=0) - member
    slot_index = lax.optimization_barrier(jnp.sum(before * member, axis=1))
    target = owner_of * capacity + slot_index
    placing = (jnp.arange(ranks * capacity, dtype=jnp.int32)[:, None] == target[None, :]).astype(jnp.float32)
    return jnp.dot(placing, blocks, precision=lax.Precision.HIGHEST)

def one_universe(pair, conv1_weight, conv1_bias, conv2_weight, conv2_bias):
    field, upstream = pair
    chans_in, deep_rows, high_rows, wide_rows = field.shape
    chan_one = conv1_weight.shape[0]
    chan_two = conv2_weight.shape[0]
    half_deep, half_high, half_wide = (deep_rows // 2, high_rows // 2, wide_rows // 2)
    padded_in = pad_field(field)
    pre_one = convolve(padded_in, conv1_weight, deep_rows, high_rows, wide_rows) + conv1_bias[:, None, None, None]
    pooled = average(leaky_relu(pre_one)).astype(jnp.bfloat16)
    padded_pool = pad_field(pooled)
    pre_two = convolve(padded_pool, conv2_weight, half_deep, half_high, half_wide) + conv2_bias[:, None, None, None]
    feature = average(leaky_relu(pre_two)).astype(jnp.bfloat16)
    delta_two = (spread_back(upstream.astype(jnp.float32)) * slope_mask(pre_two)).astype(jnp.bfloat16)
    flat_two = delta_two.reshape(chan_two, -1)
    grad_w2 = weight_grad(flat_two, padded_pool, half_deep, half_high, half_wide)
    grad_b2 = lax.optimization_barrier(jnp.sum(flat_two.astype(jnp.float32), axis=1))
    back_pooled = input_grad(pad_field(delta_two), conv2_weight, chan_one, half_deep, half_high, half_wide)
    delta_one = (spread_back(back_pooled) * slope_mask(pre_one)).astype(jnp.bfloat16)
    flat_one = delta_one.reshape(chan_one, -1)
    grad_w1 = weight_grad(flat_one, padded_in, deep_rows, high_rows, wide_rows)
    grad_b1 = lax.optimization_barrier(jnp.sum(flat_one.astype(jnp.float32), axis=1))
    vector = jnp.concatenate([grad_w1.reshape(-1), grad_b1, grad_w2.reshape(-1), grad_b2])
    return (feature, vector)

def reference(universe, cotangent, conv1_weight, conv1_bias, conv2_weight, conv2_bias, owners, accumulated):

    def step_one(pair):
        return one_universe(pair, conv1_weight, conv1_bias, conv2_weight, conv2_bias)
    features, vectors = lax.map(step_one, (universe, cotangent))
    totals = lax.optimization_barrier(jnp.sum(vectors, axis=0))
    blocks = jnp.pad(totals, (0, NB * 128 - totals.shape[0])).reshape(NB, 128)
    owned = accumulated + place_blocks(owners, blocks, N_DP, CAP)
    return (features, owned)
```

```python
import jax
import jax.numpy as jnp
from jax import lax
from jax.sharding import PartitionSpec as P

NB = 460


SLOPE = 0.3
OFFSETS = [
    (first, second, third) for first in range(3) for second in range(3) for third in range(3)
]


def with_halo(block, sides, width):
    for axis, dim in sides:
        count = lax.axis_size(axis)
        forward = [(i, i + 1) for i in range(count - 1)]
        forward.append((count - 1, 0))
        backward = [(target, source) for source, target in forward]
        low = lax.ppermute(
            lax.slice_in_dim(block, block.shape[dim] - width, None, axis=dim), axis, forward
        )
        high = lax.ppermute(lax.slice_in_dim(block, 0, width, axis=dim), axis, backward)
        block = jnp.concatenate([low, block, high], axis=dim)
    return block


def pad_sides(field):
    return jnp.pad(field, ((0, 0), (0, 0), (1, 1), (1, 1)))


def tap_stack(padded, deep_rows, high_rows, wide_rows, flipped):
    pieces = [
        padded[:, first : first + deep_rows, second : second + high_rows, third : third + wide_rows]
        for first, second, third in OFFSETS
    ]
    if flipped:
        pieces = pieces[::-1]
    stacked = jnp.stack(pieces, axis=0)
    return stacked.reshape(27 * padded.shape[0], deep_rows * high_rows * wide_rows)


def average(field):
    chans, deep_rows, high_rows, wide_rows = field.shape
    return field.reshape(chans, deep_rows // 2, 2, high_rows // 2, 2, wide_rows // 2, 2).mean(
        axis=(2, 4, 6)
    )


def spread_back(field):
    return jnp.repeat(jnp.repeat(jnp.repeat(field, 2, axis=1), 2, axis=2), 2, axis=3) * 0.125


def leaky_relu(value):
    return jnp.where(value > 0, value, SLOPE * value)


def slope_mask(value):
    return jnp.where(value > 0, 1.0, SLOPE)


def placing_matrix(owners, ranks, pitch):
    owner_of = owners[:, 0]
    member = (owner_of[:, None] == jnp.arange(ranks, dtype=jnp.int32)[None, :]).astype(jnp.int32)
    before = jnp.cumsum(member, axis=0) - member
    slot_index = jnp.sum(before * member, axis=1)
    target = owner_of * pitch + slot_index
    return (jnp.arange(ranks * pitch, dtype=jnp.int32)[:, None] == target[None, :]).astype(
        jnp.float32
    )


def exchange(rows, axis):
    return lax.all_to_all(rows, axis, 0, 0, tiled=True)


def sum_to_owners(placed, ranks, slabs, share):
    width = placed.shape[1]
    mine = exchange(placed, "dp").reshape(ranks, -1, width).sum(axis=0)
    mine = jnp.pad(mine, ((0, slabs * share - mine.shape[0]), (0, 0)))
    part = exchange(mine, "slab").reshape(slabs, share, width).sum(axis=0)
    return exchange(jnp.tile(part, (slabs, 1)), "slab")


def body(
    universe, cotangent, conv1_weight, conv1_bias, conv2_weight, conv2_bias, owners, accumulated
):
    field = universe[0]
    chans_in, deep_rows, high_rows, wide_rows = field.shape
    chan_one = conv1_weight.shape[0]
    chan_two = conv2_weight.shape[0]
    half_deep, half_high, half_wide = (deep_rows // 2, high_rows // 2, wide_rows // 2)
    extended = with_halo(field, (("slab", 1),), 1)
    cols_one = tap_stack(pad_sides(extended), deep_rows, high_rows, wide_rows, False)
    pre_one = (
        jnp.dot(conv1_weight, cols_one, preferred_element_type=jnp.float32) + conv1_bias[:, None]
    )
    pre_one = pre_one.reshape(chan_one, deep_rows, high_rows, wide_rows)
    pooled = average(leaky_relu(pre_one)).astype(jnp.bfloat16)
    rimmed = with_halo(pooled, (("slab", 1),), 1)
    cols_two = tap_stack(pad_sides(rimmed), half_deep, half_high, half_wide, False)
    pre_two = (
        jnp.dot(conv2_weight, cols_two, preferred_element_type=jnp.float32) + conv2_bias[:, None]
    )
    pre_two = pre_two.reshape(chan_two, half_deep, half_high, half_wide)
    feature = average(leaky_relu(pre_two)).astype(jnp.bfloat16)
    delta_two = (spread_back(cotangent[0].astype(jnp.float32)) * slope_mask(pre_two)).astype(
        jnp.bfloat16
    )
    flat_two = delta_two.reshape(chan_two, -1)
    grad_w2 = jnp.einsum("oc,kc->ok", flat_two, cols_two, preferred_element_type=jnp.float32)
    grad_b2 = jnp.sum(flat_two.astype(jnp.float32), axis=1)
    delta_rim = with_halo(delta_two, (("slab", 1),), 1)
    cols_back = tap_stack(pad_sides(delta_rim), half_deep, half_high, half_wide, True)
    weight_back = (
        conv2_weight.reshape(chan_two, 27, chan_one)
        .transpose(2, 1, 0)
        .reshape(chan_one, 27 * chan_two)
    )
    back_pooled = jnp.dot(weight_back, cols_back, preferred_element_type=jnp.float32)
    back_pooled = back_pooled.reshape(chan_one, half_deep, half_high, half_wide)
    delta_one = (spread_back(back_pooled) * slope_mask(pre_one)).astype(jnp.bfloat16)
    flat_one = delta_one.reshape(chan_one, -1)
    grad_w1 = jnp.einsum("oc,kc->ok", flat_one, cols_one, preferred_element_type=jnp.float32)
    grad_b1 = jnp.sum(flat_one.astype(jnp.float32), axis=1)
    vector = jnp.concatenate([grad_w1.reshape(-1), grad_b1, grad_w2.reshape(-1), grad_b2])
    blocks = jnp.pad(vector, (0, NB * 128 - vector.shape[0])).reshape(NB, 128)
    ranks, slabs = lax.axis_size("dp"), lax.axis_size("slab")
    capacity = accumulated.shape[0]
    pitch = -(-capacity // 16) * 16
    placing = placing_matrix(owners, ranks, pitch)
    placed = jnp.dot(placing, blocks, precision=lax.Precision.HIGHEST)
    totals = sum_to_owners(placed, ranks, slabs, -(-pitch // slabs))
    owned = accumulated + totals[:capacity]
    return (feature[None], owned)


def solution(mesh):
    in_specs = (
        P("dp", None, "slab", None, None),
        P("dp", None, "slab", None, None),
        P(),
        P(),
        P(),
        P(),
        P(),
        P("dp", None),
    )
    out_specs = (P("dp", None, "slab", None, None), P("dp", None))
    return jax.shard_map(body, mesh=mesh, in_specs=in_specs, out_specs=out_specs, check_vma=False)
```

```python
import jax
import jax.numpy as jnp
import numpy as np
from jax import lax
from jax.experimental import pallas as pl
from jax.experimental.pallas import tpu as pltpu
from jax.sharding import PartitionSpec as P

NB = 460
NB_PAD = 512
SLOPE = 0.3
BF16 = jnp.bfloat16
F32 = jnp.float32
VMEM_LIMIT = 48 * 1024 * 1024


def tap_selection():
    select = np.zeros((108, 384), np.float32)
    for first in range(3):
        for second in range(3):
            for third in range(3):
                for chan in range(4):
                    lane = (third * 16 + chan * 4 + second - 1) % 128
                    select[(9 * first + 3 * second + third) * 4 + chan, first * 128 + lane] = 1.0
    return select


def dot(left, right, precision=None):
    return jnp.dot(left, right, preferred_element_type=F32, precision=precision)


def dot_lanes(left, right):
    return lax.dot_general(left, right, (((1,), (1,)), ((), ())), preferred_element_type=F32)


def lanes_of(shape):
    return lax.broadcasted_iota(jnp.int32, shape, 1)


def turned(value, shift):
    shift = shift % 128
    return pltpu.roll(value, shift, 1) if shift else value


def from_left(value):
    return jnp.where(lanes_of(value.shape) == 0, 0.0, pltpu.roll(value, 1, 1))


def from_right(value):
    return jnp.where(lanes_of(value.shape) == 127, 0.0, pltpu.roll(value, 127, 1))


def leaky_relu(value):
    return jnp.where(value > 0, value, SLOPE * value)


def slope_mask(value):
    return jnp.where(value > 0, 1.0, SLOPE)


def weights_kernel(w1_ref, select_ref, w2_ref, big1_ref, big2_ref, back_ref, comb_ref):
    base = dot(w1_ref[...], select_ref[...])
    y_of = lanes_of((32, 128)) % 4
    for y in range(4):
        near = jnp.abs(y_of - y) <= 1
        for r in range(4):
            for first in range(3):
                part = turned(base[:, first * 128 : first * 128 + 128], r * 16 + y)
                big1_ref[(y * 4 + r) * 32 : (y * 4 + r) * 32 + 32, first * 128 : first * 128 + 128] = (
                    jnp.where(near, part, 0.0).astype(BF16)
                )
    group = lanes_of((64, 128)) // 32

    def gathered(taps):
        result = jnp.zeros((64, 128), F32)
        for place, tap in enumerate(taps):
            if tap is not None:
                column = w2_ref[:, tap // 4 * 128 : tap // 4 * 128 + 128].astype(F32)
                result = jnp.where(group == place, turned(column, (place - tap) * 32), result)
        return result

    for first in range(3):
        for second in range(3):
            for ph in range(2):
                taps = [
                    (first * 3 + second) * 3 + col - ph if 0 <= col - ph <= 2 else None
                    for col in range(4)
                ]
                tile = gathered(taps).astype(BF16)
                for y in range(2):
                    other = y + second - 1
                    if 0 <= other < 2:
                        big2_ref[
                            (y * 2 + ph) * 64 : (y * 2 + ph) * 64 + 64,
                            first * 256 + other * 128 : first * 256 + other * 128 + 128,
                        ] = tile
    for first in range(3):
        for other in range(2):
            for pair in range(2):
                tiles = []
                for col in (2 * pair, 2 * pair + 1):
                    taps = [
                        ((2 - first) * 3 + 1 - (other - y)) * 3 + 2 - (col - ph)
                        if 0 <= col - ph <= 2
                        else None
                        for y in range(2)
                        for ph in range(2)
                    ]
                    tiles.append(gathered(taps))
                at = first * 512 + other * 256 + pair * 128
                back_ref[:, at : at + 128] = jnp.concatenate(tiles, axis=0).T.astype(BF16)
    for col in range(6):
        cell = lax.broadcasted_iota(jnp.int32, (512, 128), 0)
        comb_ref[:, col * 128 : col * 128 + 128] = jnp.where(
            cell == 4 * lanes_of((512, 128)) + col - 1, 1.0, 0.0
        ).astype(BF16)


def main_kernel(
    prev_ref,
    own_ref,
    next_ref,
    after_ref,
    big1_ref,
    big2_ref,
    back_ref,
    comb_ref,
    bias1_ref,
    bias2_ref,
    target_ref,
    select_ref,
    feature_ref,
    placed_ref,
    field_ref,
    pooled_ref,
    delta2_ref,
    pre_ref,
    delta1_ref,
    blocks_ref,
    order_ref,
):
    source = jnp.concatenate(
        [prev_ref[16:64, :], own_ref[0:64, :], next_ref[0:64, :], after_ref[0:48, :]], axis=0
    )
    for layer in range(14):
        field_ref[layer * 128 + 96 : layer * 128 + 128, :] = jnp.zeros((32, 128), BF16)
    for col in range(6):
        part = dot(source, comb_ref[:, col * 128 : col * 128 + 128]).astype(BF16)
        for layer in range(14):
            at = layer * 128 + col * 16
            field_ref[at : at + 16, :] = part[layer * 16 : layer * 16 + 16, :]

    bias1 = jnp.broadcast_to(bias1_ref[...], (32, 128))
    for half in range(6):
        sums = [None] * 4
        for deep in range(2):
            at = (2 * half + deep) * 128
            conv = dot(big1_ref[...], field_ref[at : at + 384, :])
            for y in range(4):
                for r in range(4):
                    block = conv[(y * 4 + r) * 32 : (y * 4 + r) * 32 + 32, :] + bias1
                    if half in (2, 3):
                        row = (2 * (half - 2) + deep) * 512 + (y * 4 + r) * 32
                        pre_ref[row : row + 32, :] = block
                    value = leaky_relu(block)
                    slot = y // 2 * 2 + r // 2
                    sums[slot] = value if sums[slot] is None else sums[slot] + value
        for y in range(2):
            even = (sums[2 * y] * 0.125).astype(BF16).astype(F32)
            odd = (sums[2 * y + 1] * 0.125).astype(BF16).astype(F32)
            at = half * 256 + y * 128
            pooled_ref[at : at + 128, :] = jnp.concatenate(
                [from_left(odd), even, odd, from_right(even)], axis=0
            ).astype(BF16)

    bias2 = jnp.broadcast_to(bias2_ref[...], (64, 128))
    total = jnp.zeros((64, 128), F32)
    for half in range(4):
        conv = dot(big2_ref[...], pooled_ref[half * 256 : half * 256 + 768, :])
        upstream_ref = own_ref if half < 2 else next_ref
        upstream = (
            jnp.concatenate(
                [upstream_ref[64:80, u * 128 : u * 128 + 128] for u in range(4)], axis=0
            ).astype(F32)
            * 0.125
        )
        for y in range(2):
            deltas = []
            for ph in range(2):
                block = conv[(y * 2 + ph) * 64 : (y * 2 + ph) * 64 + 64, :] + bias2
                if half < 2:
                    total = total + leaky_relu(block)
                deltas.append((upstream * slope_mask(block)).astype(BF16).astype(F32))
            at = half * 512 + y * 256
            delta2_ref[at : at + 256, :] = jnp.concatenate(
                [from_left(deltas[1]), deltas[0], deltas[1], from_right(deltas[0])], axis=0
            ).astype(BF16)
    feature = total * 0.125
    for u in range(4):
        order_ref[pl.ds(u, 16, stride=4), :] = feature[u * 16 : u * 16 + 16, :]
    feature_ref[...] = order_ref[...].astype(BF16)

    ones = jnp.ones((8, 128), BF16)
    grad2 = None
    bias_sum2 = None
    for half in (1, 2):
        delta = jnp.concatenate(
            [
                delta2_ref[half * 512 + 64 : half * 512 + 192, :],
                delta2_ref[half * 512 + 320 : half * 512 + 448, :],
            ],
            axis=0,
        )
        term = dot_lanes(delta, pooled_ref[half * 256 : half * 256 + 768, :])
        bias_term = dot_lanes(ones, delta)
        grad2 = term if grad2 is None else grad2 + term
        bias_sum2 = bias_term if bias_sum2 is None else bias_sum2 + bias_term

    grad1 = None
    bias_sum1 = None
    for half in (1, 2):
        back = dot(back_ref[...], delta2_ref[(half - 1) * 512 : (half + 2) * 512, :]) * 0.125
        for deep in range(2):
            number = 2 * (half - 1) + deep
            for y in range(4):
                for r in range(4):
                    row = number * 512 + (y * 4 + r) * 32
                    slot = (y // 2 * 2 + r // 2) * 32
                    delta1_ref[row : row + 32, :] = (
                        back[slot : slot + 32, :] * slope_mask(pre_ref[row : row + 32, :])
                    ).astype(BF16)
            delta = delta1_ref[number * 512 : number * 512 + 512, :]
            at = (number + 4) * 128
            term = dot_lanes(delta, field_ref[at : at + 384, :])
            bias_term = dot_lanes(ones, delta)
            grad1 = term if grad1 is None else grad1 + term
            bias_sum1 = bias_term if bias_sum1 is None else bias_sum1 + bias_term

    exact = lax.Precision.HIGHEST
    q = lax.broadcasted_iota(jnp.int32, (512, 128), 0)
    bias_row1 = dot(bias_sum1, jnp.where(q % 32 == lanes_of((512, 128)), 1.0, 0.0), exact)
    q = lax.broadcasted_iota(jnp.int32, (256, 128), 0)
    lane = 32 + 4 * (q % 16) + q % 64 // 16
    bias_row2 = dot(bias_sum2, jnp.where(lane == lanes_of((256, 128)), 1.0, 0.0), exact)

    y_of = lanes_of((32, 128)) % 4
    parts = []
    for first in range(3):
        part = jnp.zeros((32, 128), F32)
        for y in range(4):
            near = jnp.abs(y_of - y) <= 1
            for r in range(4):
                row = (y * 4 + r) * 32
                block = grad1[row : row + 32, first * 128 : first * 128 + 128]
                part = part + turned(jnp.where(near, block, 0.0), -(r * 16 + y))
        parts.append(part)
    flat1 = dot(jnp.concatenate(parts, axis=1), select_ref[...], exact)
    rows = [None] * 28
    lane8 = lanes_of((8, 128))
    for o in range(32):
        begin = o * 108 // 128
        shift = o * 108 % 128
        moved = turned(flat1[o // 8 * 8 : o // 8 * 8 + 8, :], shift)
        for row, kept in ((begin, lane8 >= shift), (begin + 1, lane8 < shift)):
            if row == begin or shift + 108 > 128:
                term = jnp.where(kept, moved, 0.0)[o % 8 : o % 8 + 1, :]
                rows[row] = term if rows[row] is None else rows[row] + term
    for row in range(27):
        blocks_ref[row : row + 1, :] = rows[row]

    taps = []
    for first in range(3):
        for second in range(3):
            part = None
            for y in range(2):
                other = y + second - 1
                if 0 <= other < 2:
                    for ph in range(2):
                        row = (y * 2 + ph) * 64
                        at = first * 256 + other * 128
                        block = turned(grad2[row : row + 64, at : at + 128], -ph * 32)
                        part = block if part is None else part + block
            taps.append(part)
    group = lanes_of((16, 128)) // 32

    def chunk(number, place):
        u, tap = (number - 1) // 27, (number - 1) % 27
        return turned(taps[tap // 3][u * 16 : u * 16 + 16, :], (place - tap % 3) * 32)

    last = pltpu.roll(chunk(108, 0), 1, 0)
    row_of = lax.broadcasted_iota(jnp.int32, (16, 128), 0)
    for k in range(27):
        if k == 0:
            value = jnp.where(row_of == 0, jnp.broadcast_to(bias_row1[0:1, :], (16, 128)), last)
        else:
            value = chunk(4 * k, 0)
        for place in range(1, 4):
            value = jnp.where(group == place, chunk(4 * k + place, place), value)
        blocks_ref[pl.ds(27 + k, 16, stride=27), :] = value
    blocks_ref[459:460, :] = jnp.where(lanes_of((1, 128)) < 32, last[0:1, :], bias_row2[0:1, :])
    blocks_ref[NB:NB_PAD, :] = jnp.zeros((NB_PAD - NB, 128), F32)

    blocks = blocks_ref[...]
    high = blocks.astype(BF16)
    rest = blocks - high.astype(F32)
    middle = rest.astype(BF16)
    low = (rest - middle.astype(F32)).astype(BF16)
    terms = jnp.concatenate([high, middle, low], axis=1)
    target = target_ref[...]
    for tile in range(placed_ref.shape[0] // 128):
        row_at = lax.broadcasted_iota(jnp.int32, (128, NB_PAD), 0) + tile * 128
        placing = jnp.where(row_at == target, 1.0, 0.0).astype(BF16)
        moved = dot(placing, terms)
        placed_ref[tile * 128 : tile * 128 + 128, :] = (
            moved[:, 0:128] + moved[:, 128:256] + moved[:, 256:384]
        )


def whole():
    return pl.BlockSpec(memory_space=pltpu.VMEM)


def expand_weights(w1, w2_padded):
    return pl.pallas_call(
        weights_kernel,
        out_shape=(
            jax.ShapeDtypeStruct((512, 384), BF16),
            jax.ShapeDtypeStruct((256, 768), BF16),
            jax.ShapeDtypeStruct((128, 1536), BF16),
            jax.ShapeDtypeStruct((512, 768), BF16),
        ),
        in_specs=[whole()] * 3,
        out_specs=(whole(),) * 4,
        compiler_params=pltpu.CompilerParams(vmem_limit_bytes=VMEM_LIMIT),
        cost_estimate=pl.CostEstimate(flops=1 << 26, bytes_accessed=4 << 20, transcendentals=0),
    )(w1, jnp.asarray(tap_selection(), BF16), w2_padded)


def forward_backward(packed, weights, bias1, bias2, target, placed_rows):
    return pl.pallas_call(
        main_kernel,
        out_shape=(
            jax.ShapeDtypeStruct((64, 128), BF16),
            jax.ShapeDtypeStruct((placed_rows, 128), F32),
        ),
        in_specs=[whole()] * 12,
        out_specs=(whole(),) * 2,
        scratch_shapes=[
            pltpu.VMEM((14 * 128, 128), BF16),
            pltpu.VMEM((6 * 256, 128), BF16),
            pltpu.VMEM((4 * 512, 128), BF16),
            pltpu.VMEM((4 * 512, 128), F32),
            pltpu.VMEM((4 * 512, 128), BF16),
            pltpu.VMEM((NB_PAD, 128), F32),
            pltpu.VMEM((64, 128), F32),
        ],
        compiler_params=pltpu.CompilerParams(vmem_limit_bytes=VMEM_LIMIT),
        cost_estimate=pl.CostEstimate(flops=1 << 31, bytes_accessed=4 << 20, transcendentals=0),
    )(
        *packed,
        *weights,
        bias1,
        bias2,
        target,
        jnp.asarray(np.pad(tap_selection().T, ((0, 0), (0, 20))), F32),
    )


def block_targets(owners, ranks, pitch):
    owner_of = owners[:, 0]
    member = (owner_of[:, None] == jnp.arange(ranks, dtype=jnp.int32)[None, :]).astype(jnp.int32)
    before = jnp.cumsum(member, axis=0) - member
    slot_index = jnp.sum(before * member, axis=1)
    target = owner_of * pitch + slot_index
    return jnp.pad(target[None, :], ((0, 0), (0, NB_PAD - NB)), constant_values=-1)


def exchange(rows, axis):
    return lax.all_to_all(rows, axis, 0, 0, tiled=True)


def sum_to_owners(placed, ranks, slabs, share):
    width = placed.shape[1]
    mine = exchange(placed, "dp").reshape(ranks, -1, width).sum(axis=0)
    mine = jnp.pad(mine, ((0, slabs * share - mine.shape[0]), (0, 0)))
    part = exchange(mine, "slab").reshape(slabs, share, width).sum(axis=0)
    return exchange(jnp.tile(part, (slabs, 1)), "slab")


def body(
    universe, cotangent, conv1_weight, conv1_bias, conv2_weight, conv2_bias, owners, accumulated
):
    ranks, slabs = lax.axis_size("dp"), lax.axis_size("slab")
    packed = jnp.concatenate(
        [universe[0].transpose(1, 0, 2, 3).reshape(64, 512), cotangent.reshape(16, 512)], axis=0
    )

    def from_slab(distance):
        pairs = [(i, (i - distance) % slabs) for i in range(slabs)]
        return lax.ppermute(packed, "slab", pairs)

    spans = (from_slab(-1), packed, from_slab(1), from_slab(2))
    w2 = conv2_weight.reshape(16, 4, 864).transpose(1, 0, 2).reshape(64, 864)
    weights = expand_weights(conv1_weight, jnp.pad(w2, ((0, 0), (0, 32))))
    bias2 = conv2_bias.reshape(16, 4).T.reshape(64, 1)
    capacity = accumulated.shape[0]
    step = max(16, 128 // ranks)
    pitch = -(-capacity // step) * step
    target = block_targets(owners, ranks, pitch)
    feature, placed = forward_backward(
        spans, weights, conv1_bias.reshape(32, 1), bias2, target, ranks * pitch
    )
    totals = sum_to_owners(placed, ranks, slabs, -(-pitch // slabs))
    owned = accumulated + totals[:capacity]
    return (feature.reshape(1, 64, 1, 1, 128), owned)


def solution(mesh):
    in_specs = (
        P("dp", None, "slab", None, None),
        P("dp", None, "slab", None, None),
        P(),
        P(),
        P(),
        P(),
        P(),
        P("dp", None),
    )
    out_specs = (P("dp", None, "slab", None, None), P("dp", None))
    return jax.shard_map(body, mesh=mesh, in_specs=in_specs, out_specs=out_specs, check_vma=False)
```

```python
import jax
import jax.numpy as jnp
import numpy as np
from jax import lax
from jax.experimental import pallas as pl
from jax.experimental.pallas import tpu as pltpu
from jax.sharding import Mesh
from jax.sharding import PartitionSpec as P

NB = 460
NB_PAD = 512
SLOPE = 0.3
BF16 = jnp.bfloat16
F32 = jnp.float32
VMEM_LIMIT = 48 * 1024 * 1024


def tap_selection():
    select = np.zeros((108, 384), np.float32)
    for first in range(3):
        for second in range(3):
            for third in range(3):
                for chan in range(4):
                    lane = (third * 16 + chan * 4 + second - 1) % 128
                    select[(9 * first + 3 * second + third) * 4 + chan, first * 128 + lane] = 1.0
    return select


def dot(left, right, precision=None):
    return jnp.dot(left, right, preferred_element_type=F32, precision=precision)


def dot_lanes(left, right):
    return lax.dot_general(left, right, (((1,), (1,)), ((), ())), preferred_element_type=F32)


def lanes_of(shape):
    return lax.broadcasted_iota(jnp.int32, shape, 1)


def turned(value, shift):
    shift = shift % 128
    return pltpu.roll(value, shift, 1) if shift else value


def from_left(value):
    return jnp.where(lanes_of(value.shape) == 0, 0.0, pltpu.roll(value, 1, 1))


def from_right(value):
    return jnp.where(lanes_of(value.shape) == 127, 0.0, pltpu.roll(value, 127, 1))


def side_by_side(ref, at, step, rows):
    return jnp.concatenate([ref[at : at + rows, :], ref[at + step : at + step + rows, :]], axis=1)


def leaky_relu(value):
    return jnp.where(value > 0, value, SLOPE * value)


def slope_mask(value):
    return jnp.where(value > 0, 1.0, SLOPE)


def channel_order():
    row = lax.broadcasted_iota(jnp.int32, (64, 64), 0)
    return jnp.where(lanes_of((64, 64)) == 4 * (row % 16) + row // 16, 1.0, 0.0)


def weights_kernel(
    rank_ref,
    w1_ref,
    select_ref,
    w2_ref,
    bias1_ref,
    bias2_ref,
    owners_ref,
    accumulated_ref,
    big1_ref,
    big2_ref,
    back_ref,
    comb_ref,
    wide1_ref,
    wide2_ref,
    target_ref,
    kept_ref,
    ordered_ref,
):
    kept_ref[...] = accumulated_ref[...]
    ordered_ref[:, 768:896] = jnp.zeros((64, 128), F32)
    ordered_ref[:, 0:864] = dot(channel_order().astype(BF16), w2_ref[...])
    place = lax.broadcasted_iota(jnp.int32, (32, 32), 0) == lanes_of((32, 32))
    column = jnp.sum(jnp.where(place, bias1_ref[...], 0.0), axis=1, keepdims=True)
    wide1_ref[...] = jnp.broadcast_to(column, (32, 128))
    column = jnp.sum(channel_order() * bias2_ref[...], axis=1, keepdims=True)
    wide2_ref[...] = jnp.broadcast_to(column, (64, 128))

    mine = owners_ref[...] == rank_ref[0]
    member = jnp.broadcast_to(jnp.where(mine, 1.0, 0.0), (8, NB)).astype(BF16)
    earlier = lax.broadcasted_iota(jnp.int32, (NB, NB), 0) < lanes_of((NB, NB))
    before = dot(member, jnp.where(earlier, 1.0, 0.0).astype(BF16))[0:1, :]
    target_ref[:, 384:NB_PAD] = jnp.full((1, 128), -1, jnp.int32)
    target_ref[:, 0:NB] = jnp.where(mine, before.astype(jnp.int32), -1)

    base = dot(w1_ref[...], select_ref[...])
    y_of = lanes_of((32, 128)) % 4
    for y in range(4):
        near = jnp.abs(y_of - y) <= 1
        for r in range(4):
            for first in range(3):
                part = turned(base[:, first * 128 : first * 128 + 128], r * 16 + y)
                big1_ref[(y * 4 + r) * 32 : (y * 4 + r) * 32 + 32, first * 128 : first * 128 + 128] = (
                    jnp.where(near, part, 0.0).astype(BF16)
                )
    group = lanes_of((64, 128)) // 32

    def gathered(taps):
        result = jnp.zeros((64, 128), F32)
        for place, tap in enumerate(taps):
            if tap is not None:
                column = ordered_ref[:, tap // 4 * 128 : tap // 4 * 128 + 128]
                result = jnp.where(group == place, turned(column, (place - tap) * 32), result)
        return result

    for first in range(3):
        for second in range(3):
            for ph in range(2):
                taps = [
                    (first * 3 + second) * 3 + col - ph if 0 <= col - ph <= 2 else None
                    for col in range(4)
                ]
                tile = gathered(taps).astype(BF16)
                for y in range(2):
                    other = y + second - 1
                    if 0 <= other < 2:
                        big2_ref[
                            (y * 2 + ph) * 64 : (y * 2 + ph) * 64 + 64,
                            first * 256 + other * 128 : first * 256 + other * 128 + 128,
                        ] = tile
    for first in range(3):
        for other in range(2):
            for pair in range(2):
                tiles = []
                for col in (2 * pair, 2 * pair + 1):
                    taps = [
                        ((2 - first) * 3 + 1 - (other - y)) * 3 + 2 - (col - ph)
                        if 0 <= col - ph <= 2
                        else None
                        for y in range(2)
                        for ph in range(2)
                    ]
                    tiles.append(gathered(taps))
                at = first * 512 + other * 256 + pair * 128
                back_ref[:, at : at + 128] = jnp.concatenate(tiles, axis=0).T.astype(BF16)
    for col in range(6):
        cell = lax.broadcasted_iota(jnp.int32, (512, 128), 0)
        comb_ref[:, col * 128 : col * 128 + 128] = jnp.where(
            cell == 4 * lanes_of((512, 128)) + col - 1, 1.0, 0.0
        ).astype(BF16)


def main_kernel(
    prev_ref,
    own_ref,
    next_ref,
    after_ref,
    big1_ref,
    big2_ref,
    back_ref,
    comb_ref,
    wide1_ref,
    wide2_ref,
    select_ref,
    feature_ref,
    blocks_ref,
    field_ref,
    pooled_ref,
    delta2_ref,
    pre_ref,
    delta1_ref,
    order_ref,
):
    source = jnp.concatenate(
        [prev_ref[16:64, :], own_ref[0:64, :], next_ref[0:64, :], after_ref[0:48, :]], axis=0
    )
    for layer in range(14):
        field_ref[layer * 128 + 96 : layer * 128 + 128, :] = jnp.zeros((32, 128), BF16)
    for col in range(6):
        part = dot(source, comb_ref[:, col * 128 : col * 128 + 128]).astype(BF16)
        for layer in range(14):
            at = layer * 128 + col * 16
            field_ref[at : at + 16, :] = part[layer * 16 : layer * 16 + 16, :]

    bias1 = wide1_ref[...]
    for half in range(6):
        sums = [None] * 4
        conv = dot(big1_ref[...], side_by_side(field_ref, 2 * half * 128, 128, 384))
        for deep in range(2):
            for y in range(4):
                for r in range(4):
                    block = (
                        conv[(y * 4 + r) * 32 : (y * 4 + r) * 32 + 32, deep * 128 : deep * 128 + 128]
                        + bias1
                    )
                    if half in (2, 3):
                        row = (2 * (half - 2) + deep) * 512 + (y * 4 + r) * 32
                        pre_ref[row : row + 32, :] = block
                    value = leaky_relu(block)
                    slot = y // 2 * 2 + r // 2
                    sums[slot] = value if sums[slot] is None else sums[slot] + value
        for y in range(2):
            even = (sums[2 * y] * 0.125).astype(BF16).astype(F32)
            odd = (sums[2 * y + 1] * 0.125).astype(BF16).astype(F32)
            at = half * 256 + y * 128
            pooled_ref[at : at + 128, :] = jnp.concatenate(
                [from_left(odd), even, odd, from_right(even)], axis=0
            ).astype(BF16)

    bias2 = wide2_ref[...]
    total = jnp.zeros((64, 128), F32)
    for half in range(4):
        if half % 2 == 0:
            conv = dot(big2_ref[...], side_by_side(pooled_ref, half * 256, 256, 768))
        lane = half % 2 * 128
        upstream_ref = own_ref if half < 2 else next_ref
        upstream = (
            jnp.concatenate(
                [upstream_ref[64:80, u * 128 : u * 128 + 128] for u in range(4)], axis=0
            ).astype(F32)
            * 0.125
        )
        for y in range(2):
            deltas = []
            for ph in range(2):
                row = (y * 2 + ph) * 64
                block = conv[row : row + 64, lane : lane + 128] + bias2
                if half < 2:
                    total = total + leaky_relu(block)
                deltas.append((upstream * slope_mask(block)).astype(BF16).astype(F32))
            at = half * 512 + y * 256
            delta2_ref[at : at + 256, :] = jnp.concatenate(
                [from_left(deltas[1]), deltas[0], deltas[1], from_right(deltas[0])], axis=0
            ).astype(BF16)
    feature = total * 0.125
    for u in range(4):
        order_ref[pl.ds(u, 16, stride=4), :] = feature[u * 16 : u * 16 + 16, :]
    feature_ref[...] = order_ref[...].astype(BF16)

    ones = jnp.ones((8, 256), BF16)
    delta = jnp.concatenate(
        [side_by_side(delta2_ref, 512 + y * 256 + 64, 512, 128) for y in range(2)], axis=0
    )
    grad2 = dot_lanes(delta, side_by_side(pooled_ref, 256, 256, 768))
    bias_sum2 = dot_lanes(ones, delta)

    backs = dot(back_ref[...], side_by_side(delta2_ref, 0, 512, 1536)) * 0.125
    grad1 = None
    bias_sum1 = None
    for half in range(2):
        for deep in range(2):
            for y in range(4):
                for r in range(4):
                    row = (2 * half + deep) * 512 + (y * 4 + r) * 32
                    slot = (y // 2 * 2 + r // 2) * 32
                    back = backs[slot : slot + 32, half * 128 : half * 128 + 128]
                    delta1_ref[row : row + 32, :] = (
                        back * slope_mask(pre_ref[row : row + 32, :])
                    ).astype(BF16)
        delta = side_by_side(delta1_ref, half * 1024, 512, 512)
        term = dot_lanes(delta, side_by_side(field_ref, (2 * half + 4) * 128, 128, 384))
        bias_term = dot_lanes(ones, delta)
        grad1 = term if grad1 is None else grad1 + term
        bias_sum1 = bias_term if bias_sum1 is None else bias_sum1 + bias_term

    exact = lax.Precision.HIGHEST
    q = lax.broadcasted_iota(jnp.int32, (512, 128), 0)
    bias_row1 = dot(bias_sum1, jnp.where(q % 32 == lanes_of((512, 128)), 1.0, 0.0), exact)
    q = lax.broadcasted_iota(jnp.int32, (256, 128), 0)
    lane = 32 + 4 * (q % 16) + q % 64 // 16
    bias_row2 = dot(bias_sum2, jnp.where(lane == lanes_of((256, 128)), 1.0, 0.0), exact)

    y_of = lanes_of((32, 128)) % 4
    parts = []
    for first in range(3):
        part = jnp.zeros((32, 128), F32)
        for y in range(4):
            near = jnp.abs(y_of - y) <= 1
            for r in range(4):
                row = (y * 4 + r) * 32
                block = grad1[row : row + 32, first * 128 : first * 128 + 128]
                part = part + turned(jnp.where(near, block, 0.0), -(r * 16 + y))
        parts.append(part)
    flat1 = dot(jnp.concatenate(parts, axis=1), select_ref[...], exact)
    rows = [None] * 28
    lane8 = lanes_of((8, 128))
    for o in range(32):
        begin = o * 108 // 128
        shift = o * 108 % 128
        moved = turned(flat1[o // 8 * 8 : o // 8 * 8 + 8, :], shift)
        for row, kept in ((begin, lane8 >= shift), (begin + 1, lane8 < shift)):
            if row == begin or shift + 108 > 128:
                term = jnp.where(kept, moved, 0.0)[o % 8 : o % 8 + 1, :]
                rows[row] = term if rows[row] is None else rows[row] + term
    for row in range(27):
        blocks_ref[row : row + 1, :] = rows[row]

    taps = []
    for first in range(3):
        for second in range(3):
            part = None
            for y in range(2):
                other = y + second - 1
                if 0 <= other < 2:
                    for ph in range(2):
                        row = (y * 2 + ph) * 64
                        at = first * 256 + other * 128
                        block = turned(grad2[row : row + 64, at : at + 128], -ph * 32)
                        part = block if part is None else part + block
            taps.append(part)
    group = lanes_of((16, 128)) // 32

    def chunk(number, place):
        u, tap = (number - 1) // 27, (number - 1) % 27
        return turned(taps[tap // 3][u * 16 : u * 16 + 16, :], (place - tap % 3) * 32)

    last = pltpu.roll(chunk(108, 0), 1, 0)
    row_of = lax.broadcasted_iota(jnp.int32, (16, 128), 0)
    for k in range(27):
        if k == 0:
            value = jnp.where(row_of == 0, jnp.broadcast_to(bias_row1[0:1, :], (16, 128)), last)
        else:
            value = chunk(4 * k, 0)
        for place in range(1, 4):
            value = jnp.where(group == place, chunk(4 * k + place, place), value)
        blocks_ref[pl.ds(27 + k, 16, stride=27), :] = value
    blocks_ref[459:460, :] = jnp.where(lanes_of((1, 128)) < 32, last[0:1, :], bias_row2[0:1, :])
    blocks_ref[NB:NB_PAD, :] = jnp.zeros((NB_PAD - NB, 128), F32)


def owned_kernel(blocks_ref, target_ref, kept_ref, feature_ref, feature_out_ref, owned_ref):
    feature_out_ref[...] = feature_ref[...]
    capacity = owned_ref.shape[0]
    rows = -(-capacity // 16) * 16
    blocks = blocks_ref[...]
    high = blocks.astype(BF16)
    rest = blocks - high.astype(F32)
    middle = rest.astype(BF16)
    low = (rest - middle.astype(F32)).astype(BF16)
    row_at = lax.broadcasted_iota(jnp.int32, (rows, NB_PAD), 0)
    placing = jnp.where(row_at == target_ref[...], 1.0, 0.0).astype(BF16)
    moved = dot(placing, jnp.concatenate([high, middle, low], axis=1))
    total = moved[:, 0:128] + moved[:, 128:256] + moved[:, 256:384]
    owned_ref[...] = kept_ref[...] + total[0:capacity, :]


def whole():
    return pl.BlockSpec(memory_space=pltpu.VMEM)


def params():
    return pltpu.CompilerParams(vmem_limit_bytes=VMEM_LIMIT)


def expand_weights(rank, w1, w2, bias1, bias2, owners, accumulated):
    return pl.pallas_call(
        weights_kernel,
        out_shape=(
            jax.ShapeDtypeStruct((512, 384), BF16),
            jax.ShapeDtypeStruct((256, 768), BF16),
            jax.ShapeDtypeStruct((128, 1536), BF16),
            jax.ShapeDtypeStruct((512, 768), BF16),
            jax.ShapeDtypeStruct((32, 128), F32),
            jax.ShapeDtypeStruct((64, 128), F32),
            jax.ShapeDtypeStruct((1, NB_PAD), jnp.int32),
            jax.ShapeDtypeStruct(accumulated.shape, F32),
        ),
        in_specs=[pl.BlockSpec(memory_space=pltpu.SMEM)] + [whole()] * 7,
        out_specs=(whole(),) * 8,
        scratch_shapes=[pltpu.VMEM((64, 896), F32)],
        compiler_params=params(),
        cost_estimate=pl.CostEstimate(flops=1 << 26, bytes_accessed=4 << 20, transcendentals=0),
    )(rank, w1, jnp.asarray(tap_selection(), BF16), w2, bias1, bias2, owners, accumulated)


def forward_backward(spans, weights):
    return pl.pallas_call(
        main_kernel,
        out_shape=(
            jax.ShapeDtypeStruct((64, 128), BF16),
            jax.ShapeDtypeStruct((NB_PAD, 128), F32),
        ),
        in_specs=[whole()] * 11,
        out_specs=(whole(),) * 2,
        scratch_shapes=[
            pltpu.VMEM((14 * 128, 128), BF16),
            pltpu.VMEM((6 * 256, 128), BF16),
            pltpu.VMEM((4 * 512, 128), BF16),
            pltpu.VMEM((4 * 512, 128), F32),
            pltpu.VMEM((4 * 512, 128), BF16),
            pltpu.VMEM((64, 128), F32),
        ],
        compiler_params=params(),
        cost_estimate=pl.CostEstimate(flops=1 << 31, bytes_accessed=4 << 20, transcendentals=0),
    )(*spans, *weights, jnp.asarray(np.pad(tap_selection().T, ((0, 0), (0, 20))), F32))


def add_owned(blocks, target, kept, feature):
    return pl.pallas_call(
        owned_kernel,
        out_shape=(
            jax.ShapeDtypeStruct(feature.shape, feature.dtype),
            jax.ShapeDtypeStruct(kept.shape, kept.dtype),
        ),
        in_specs=[whole()] * 4,
        out_specs=(whole(),) * 2,
        compiler_params=params(),
        cost_estimate=pl.CostEstimate(flops=1 << 27, bytes_accessed=1 << 20, transcendentals=0),
    )(blocks, target, kept, feature)


SLAB = ("z_hi", "y", "core")
DP = ("z_lo", "x")
PLANE = ("x", "z_hi", "z_lo")
REST = ("y", "core")


def exchange(rows, axes):
    return lax.all_to_all(rows, axes, 0, 0, tiled=True)


def sum_everywhere(blocks):
    width = blocks.shape[1]
    plane, rest = lax.axis_size(PLANE), lax.axis_size(REST)
    part = exchange(blocks, PLANE).reshape(plane, -1, width).sum(axis=0)
    part = exchange(jnp.tile(part, (rest, 1)), REST).reshape(rest, -1, width).sum(axis=0)
    return exchange(jnp.tile(part, (plane, 1)), PLANE)


def body(
    universe, cotangent, conv1_weight, conv1_bias, conv2_weight, conv2_bias, owners, accumulated
):
    slabs = lax.axis_size(SLAB)
    packed = jnp.concatenate(
        [universe[0].transpose(1, 0, 2, 3).reshape(64, 512), cotangent.reshape(16, 512)], axis=0
    )

    def from_slab(distance):
        pairs = [(i, (i - distance) % slabs) for i in range(slabs)]
        return lax.ppermute(packed, SLAB, pairs)

    spans = (from_slab(-1), packed, from_slab(1), from_slab(2))
    *weights, target, kept = expand_weights(
        lax.axis_index(DP).reshape(1),
        conv1_weight,
        conv2_weight,
        conv1_bias.reshape(1, 32),
        conv2_bias.reshape(1, 64),
        owners.reshape(1, NB),
        accumulated,
    )
    feature, blocks = forward_backward(spans, weights)
    feature, owned = add_owned(sum_everywhere(blocks), target, kept, feature)
    return (feature.reshape(1, 64, 1, 1, 128), owned)


def split_mesh(mesh):
    slabs, ranks = mesh.devices.shape
    x = min(4, ranks)
    y = min(8, slabs // 2)
    shape = (slabs // (2 * y), y, 2, ranks // x, x)
    return Mesh(mesh.devices.reshape(shape), SLAB + DP)


def solution(mesh):
    in_specs = (
        P(DP, None, SLAB, None, None),
        P(DP, None, SLAB, None, None),
        P(),
        P(),
        P(),
        P(),
        P(),
        P(DP, None),
    )
    out_specs = (P(DP, None, SLAB, None, None), P(DP, None))
    return jax.shard_map(
        body, mesh=split_mesh(mesh), in_specs=in_specs, out_specs=out_specs, check_vma=False
    )
```

```python
import jax
import jax.numpy as jnp
import numpy as np
from jax import lax
from jax.experimental import pallas as pl
from jax.experimental.pallas import tpu as pltpu
from jax.sharding import Mesh
from jax.sharding import PartitionSpec as P

NB = 460
NB_PAD = 512
SLOPE = 0.3
BF16 = jnp.bfloat16
F32 = jnp.float32
VMEM_LIMIT = 48 * 1024 * 1024


def tap_selection():
    select = np.zeros((108, 256), np.float32)
    for first in range(3):
        for second in range(3):
            for third in range(3):
                for chan in range(4):
                    lane = (first % 2 * 64 + third * 16 + chan * 4 + second - 1) % 128
                    row = (9 * first + 3 * second + third) * 4 + chan
                    select[row, first // 2 * 128 + lane] = 1.0
    return select


def dot(left, right, precision=None):
    return jnp.dot(left, right, preferred_element_type=F32, precision=precision)


def dot_lanes(left, right):
    return lax.dot_general(left, right, (((1,), (1,)), ((), ())), preferred_element_type=F32)


def lanes_of(shape):
    return lax.broadcasted_iota(jnp.int32, shape, 1)


def turned(value, shift):
    shift = shift % 128
    return pltpu.roll(value, shift, 1) if shift else value


def from_left(value):
    return jnp.where(lanes_of(value.shape) == 0, 0.0, pltpu.roll(value, 1, 1))


def from_right(value):
    return jnp.where(lanes_of(value.shape) == 127, 0.0, pltpu.roll(value, 127, 1))


def side_by_side(ref, at, step, rows):
    return jnp.concatenate([ref[at : at + rows, :], ref[at + step : at + step + rows, :]], axis=1)


def leaky_relu(value):
    return jnp.where(value > 0, value, SLOPE * value)


def slope_mask(value):
    return jnp.where(value > 0, 1.0, SLOPE)


def channel_order():
    row = lax.broadcasted_iota(jnp.int32, (64, 64), 0)
    return jnp.where(lanes_of((64, 64)) == 4 * (row % 16) + row // 16, 1.0, 0.0)


def pack_kernel(
    universe_hbm, cotangent_hbm, own_ref, late_ref, early_ref, universe_ref, cotangent_ref, sems
):
    first = pltpu.make_async_copy(universe_hbm, universe_ref, sems.at[0])
    second = pltpu.make_async_copy(cotangent_hbm, cotangent_ref, sems.at[1])
    first.start()
    second.start()
    first.wait()
    for deep in range(4):
        rows = jnp.concatenate(
            [universe_ref[0, chan, deep].astype(F32) for chan in range(4)], axis=0
        ).astype(BF16)
        own_ref[deep * 16 : deep * 16 + 16, :] = rows
        if deep > 0:
            late_ref[deep * 16 - 16 : deep * 16, :] = rows
        if deep < 3:
            early_ref[deep * 16 : deep * 16 + 16, :] = rows
    second.wait()
    for group in range(4):
        own_ref[64:80, group * 128 : group * 128 + 128] = cotangent_ref[
            group * 16 : group * 16 + 16, :
        ]


def weights_kernel(
    rank_ref,
    w1_ref,
    select_ref,
    w2_ref,
    bias1_ref,
    bias2_ref,
    owners_ref,
    accumulated_ref,
    big1_ref,
    big2_ref,
    back_ref,
    comb_ref,
    wide1_ref,
    wide2_ref,
    target_ref,
    kept_ref,
    ordered_ref,
):
    kept_ref[...] = accumulated_ref[...]
    ordered_ref[:, 768:896] = jnp.zeros((64, 128), F32)
    ordered_ref[:, 0:864] = dot(channel_order().astype(BF16), w2_ref[...])
    place = lax.broadcasted_iota(jnp.int32, (32, 32), 0) == lanes_of((32, 32))
    column = jnp.sum(jnp.where(place, bias1_ref[...], 0.0), axis=1, keepdims=True)
    wide1_ref[...] = jnp.broadcast_to(column, (32, 128))
    column = jnp.sum(channel_order() * bias2_ref[...], axis=1, keepdims=True)
    wide2_ref[...] = jnp.broadcast_to(column, (64, 128))

    mine = owners_ref[...] == rank_ref[0]
    member = jnp.broadcast_to(jnp.where(mine, 1.0, 0.0), (8, NB)).astype(BF16)
    earlier = lax.broadcasted_iota(jnp.int32, (NB, NB), 0) < lanes_of((NB, NB))
    before = dot(member, jnp.where(earlier, 1.0, 0.0).astype(BF16))[0:1, :]
    target_ref[:, 384:NB_PAD] = jnp.full((1, 128), -1, jnp.int32)
    target_ref[:, 0:NB] = jnp.where(mine, before.astype(jnp.int32), -1)

    base = dot(w1_ref[...], select_ref[...])
    y_of = lanes_of((32, 128)) % 4
    for y in range(4):
        near = jnp.abs(y_of - y) <= 1
        for r in range(2):
            for at in (0, 128):
                part = turned(base[:, at : at + 128], r * 16 + y)
                big1_ref[(y * 2 + r) * 32 : (y * 2 + r) * 32 + 32, at : at + 128] = jnp.where(
                    near, part, 0.0
                ).astype(BF16)
    group = lanes_of((64, 128)) // 32

    def gathered(taps):
        result = jnp.zeros((64, 128), F32)
        for place, tap in enumerate(taps):
            if tap is not None:
                column = ordered_ref[:, tap // 4 * 128 : tap // 4 * 128 + 128]
                result = jnp.where(group == place, turned(column, (place - tap) * 32), result)
        return result

    for first in range(3):
        for second in range(3):
            for ph in range(2):
                taps = [
                    (first * 3 + second) * 3 + col - ph if 0 <= col - ph <= 2 else None
                    for col in range(4)
                ]
                tile = gathered(taps).astype(BF16)
                for y in range(2):
                    other = y + second - 1
                    if 0 <= other < 2:
                        big2_ref[
                            (y * 2 + ph) * 64 : (y * 2 + ph) * 64 + 64,
                            first * 256 + other * 128 : first * 256 + other * 128 + 128,
                        ] = tile
    for first in range(3):
        for other in range(2):
            for pair in range(2):
                tiles = []
                for col in (2 * pair, 2 * pair + 1):
                    taps = [
                        ((2 - first) * 3 + 1 - (other - y)) * 3 + 2 - (col - ph)
                        if 0 <= col - ph <= 2
                        else None
                        for y in range(2)
                        for ph in range(2)
                    ]
                    tiles.append(gathered(taps))
                at = first * 512 + other * 256 + pair * 128
                back_ref[:, at : at + 128] = jnp.concatenate(tiles, axis=0).T.astype(BF16)
    for col in range(6):
        cell = lax.broadcasted_iota(jnp.int32, (512, 128), 0)
        comb_ref[:, col * 128 : col * 128 + 128] = jnp.where(
            cell == 4 * lanes_of((512, 128)) + col - 1, 1.0, 0.0
        ).astype(BF16)


def main_kernel(
    prev_ref,
    own_ref,
    next_ref,
    after_ref,
    big1_ref,
    big2_ref,
    back_ref,
    comb_ref,
    wide1_ref,
    wide2_ref,
    select_ref,
    feature_ref,
    blocks_ref,
    field_ref,
    pooled_ref,
    delta2_ref,
    pre_ref,
    delta1_ref,
    order_ref,
):
    source = jnp.concatenate(
        [prev_ref[...], own_ref[0:64, :], next_ref[0:64, :], after_ref[...]], axis=0
    )
    for col in range(6):
        part = dot(source, comb_ref[:, col * 128 : col * 128 + 128]).astype(BF16)
        for layer in range(14):
            at = layer * 96 + col * 16
            field_ref[at : at + 16, :] = part[layer * 16 : layer * 16 + 16, :]
    empty = jnp.zeros((64, 128), BF16)

    def around(half):
        parts = []
        for deep in range(2):
            for pair in range(2):
                at = (2 * half + deep) * 96 + pair * 32
                layers = [field_ref[at + first * 96 : at + first * 96 + 64, :] for first in range(3)]
                parts.append(jnp.concatenate(layers + [empty], axis=0))
        return jnp.concatenate(parts, axis=1)

    bias1 = wide1_ref[...]
    for half in range(6):
        conv = dot(big1_ref[...], around(half))
        for y in range(2):
            means = []
            for pair in range(2):
                total = None
                for deep in range(2):
                    lane = (deep * 2 + pair) * 128
                    for row in range(y * 128, y * 128 + 128, 32):
                        block = conv[row : row + 32, lane : lane + 128] + bias1
                        if half in (2, 3):
                            at = (half - 2) * 256 + row
                            pre_ref[at : at + 32, lane : lane + 128] = block
                        value = leaky_relu(block)
                        total = value if total is None else total + value
                means.append((total * 0.125).astype(BF16).astype(F32))
            even, odd = means
            at = half * 256 + y * 128
            pooled_ref[at : at + 128, :] = jnp.concatenate(
                [from_left(odd), even, odd, from_right(even)], axis=0
            ).astype(BF16)

    bias2 = wide2_ref[...]
    total = jnp.zeros((64, 128), F32)
    plain = jnp.concatenate(
        [
            jnp.concatenate([ref[64:80, g * 128 : g * 128 + 128] for g in range(4)], axis=0)
            for ref in (own_ref, next_ref)
        ],
        axis=1,
    )
    upstreams = dot(channel_order().astype(BF16), plain) * 0.125
    for half in range(4):
        if half % 2 == 0:
            conv = dot(big2_ref[...], side_by_side(pooled_ref, half * 256, 256, 768))
        lane = half % 2 * 128
        upstream = upstreams[:, half // 2 * 128 : half // 2 * 128 + 128]
        for y in range(2):
            deltas = []
            for ph in range(2):
                row = (y * 2 + ph) * 64
                block = conv[row : row + 64, lane : lane + 128] + bias2
                if half < 2:
                    total = total + leaky_relu(block)
                deltas.append((upstream * slope_mask(block)).astype(BF16).astype(F32))
            at = half * 512 + y * 256
            delta2_ref[at : at + 256, :] = jnp.concatenate(
                [from_left(deltas[1]), deltas[0], deltas[1], from_right(deltas[0])], axis=0
            ).astype(BF16)
    feature = total * 0.125
    for u in range(4):
        order_ref[pl.ds(u, 16, stride=4), :] = feature[u * 16 : u * 16 + 16, :]
    feature_ref[...] = order_ref[...].astype(BF16)

    ones = jnp.ones((8, 256), BF16)
    delta = jnp.concatenate(
        [side_by_side(delta2_ref, 512 + y * 256 + 64, 512, 128) for y in range(2)], axis=0
    )
    grad2 = dot_lanes(delta, side_by_side(pooled_ref, 256, 256, 768))
    bias_sum2 = dot_lanes(ones, delta)

    backs = dot(back_ref[...], side_by_side(delta2_ref, 0, 512, 1536)) * 0.125
    ones = jnp.ones((8, 512), BF16)
    grad1 = None
    bias_sum1 = None
    for half in range(2):
        for deep in range(2):
            for pair in range(2):
                lane = (deep * 2 + pair) * 128
                for row in range(0, 256, 32):
                    slot = (row // 128 * 2 + pair) * 32
                    back = backs[slot : slot + 32, half * 128 : half * 128 + 128]
                    at = half * 256 + row
                    delta1_ref[at : at + 32, lane : lane + 128] = (
                        back * slope_mask(pre_ref[at : at + 32, lane : lane + 128])
                    ).astype(BF16)
        delta = delta1_ref[half * 256 : half * 256 + 256, :]
        term = dot_lanes(delta, around(half + 2))
        bias_term = dot_lanes(ones, delta)
        grad1 = term if grad1 is None else grad1 + term
        bias_sum1 = bias_term if bias_sum1 is None else bias_sum1 + bias_term

    exact = lax.Precision.HIGHEST
    bias_row1 = bias_sum1[:, 0:128] + bias_sum1[:, 128:256]
    bias_row1 = bias_row1 + turned(bias_row1, 64)
    bias_row1 = bias_row1 + turned(bias_row1, 32)
    q = lax.broadcasted_iota(jnp.int32, (128, 128), 0)
    lane = 32 + 4 * (q % 16) + q % 64 // 16
    bias_row2 = dot(
        bias_sum2[:, 0:128] + bias_sum2[:, 128:256],
        jnp.where(lane == lanes_of((128, 128)), 1.0, 0.0),
        exact,
    )

    y_of = lanes_of((32, 128)) % 4
    parts = []
    for at in (0, 128):
        part = jnp.zeros((32, 128), F32)
        for y in range(4):
            near = jnp.abs(y_of - y) <= 1
            for r in range(2):
                row = (y * 2 + r) * 32
                block = grad1[row : row + 32, at : at + 128]
                part = part + turned(jnp.where(near, block, 0.0), -(r * 16 + y))
        parts.append(part)
    flat1 = dot(jnp.concatenate(parts, axis=1), select_ref[...], exact)
    rows = [None] * 28
    lane8 = lanes_of((8, 128))
    for o in range(32):
        begin = o * 108 // 128
        shift = o * 108 % 128
        moved = turned(flat1[o // 8 * 8 : o // 8 * 8 + 8, :], shift)
        for row, kept in ((begin, lane8 >= shift), (begin + 1, lane8 < shift)):
            if row == begin or shift + 108 > 128:
                term = jnp.where(kept, moved, 0.0)[o % 8 : o % 8 + 1, :]
                rows[row] = term if rows[row] is None else rows[row] + term
    for row in range(27):
        blocks_ref[row : row + 1, :] = rows[row]

    taps = []
    for first in range(3):
        for second in range(3):
            part = None
            for y in range(2):
                other = y + second - 1
                if 0 <= other < 2:
                    for ph in range(2):
                        row = (y * 2 + ph) * 64
                        at = first * 256 + other * 128
                        block = turned(grad2[row : row + 64, at : at + 128], -ph * 32)
                        part = block if part is None else part + block
            taps.append(part)
    group = lanes_of((16, 128)) // 32

    def chunk(number, place):
        u, tap = (number - 1) // 27, (number - 1) % 27
        return turned(taps[tap // 3][u * 16 : u * 16 + 16, :], (place - tap % 3) * 32)

    last = pltpu.roll(chunk(108, 0), 1, 0)
    row_of = lax.broadcasted_iota(jnp.int32, (16, 128), 0)
    for k in range(27):
        if k == 0:
            value = jnp.where(row_of == 0, jnp.broadcast_to(bias_row1[0:1, :], (16, 128)), last)
        else:
            value = chunk(4 * k, 0)
        for place in range(1, 4):
            value = jnp.where(group == place, chunk(4 * k + place, place), value)
        blocks_ref[pl.ds(27 + k, 16, stride=27), :] = value
    blocks_ref[459:460, :] = jnp.where(lanes_of((1, 128)) < 32, last[0:1, :], bias_row2[0:1, :])
    blocks_ref[NB:NB_PAD, :] = jnp.zeros((NB_PAD - NB, 128), F32)


def owned_kernel(blocks_ref, target_ref, kept_ref, feature_ref, feature_out_ref, owned_ref):
    feature_out_ref[...] = feature_ref[...]
    capacity = owned_ref.shape[0]
    rows = -(-capacity // 16) * 16
    blocks = blocks_ref[...]
    high = blocks.astype(BF16)
    rest = blocks - high.astype(F32)
    middle = rest.astype(BF16)
    low = (rest - middle.astype(F32)).astype(BF16)
    row_at = lax.broadcasted_iota(jnp.int32, (rows, NB_PAD), 0)
    placing = jnp.where(row_at == target_ref[...], 1.0, 0.0).astype(BF16)
    moved = dot(placing, jnp.concatenate([high, middle, low], axis=1))
    total = moved[:, 0:128] + moved[:, 128:256] + moved[:, 256:384]
    owned_ref[...] = kept_ref[...] + total[0:capacity, :]


def whole():
    return pl.BlockSpec(memory_space=pltpu.VMEM)


def params():
    return pltpu.CompilerParams(vmem_limit_bytes=VMEM_LIMIT)


def pack(universe, cotangent):
    return pl.pallas_call(
        pack_kernel,
        out_shape=(
            jax.ShapeDtypeStruct((80, 512), BF16),
            jax.ShapeDtypeStruct((48, 512), BF16),
            jax.ShapeDtypeStruct((48, 512), BF16),
        ),
        in_specs=[pl.BlockSpec(memory_space=pltpu.HBM)] * 2,
        out_specs=(whole(),) * 3,
        scratch_shapes=[
            pltpu.VMEM(universe.shape, BF16),
            pltpu.VMEM(cotangent.shape, BF16),
            pltpu.SemaphoreType.DMA((2,)),
        ],
        compiler_params=params(),
        cost_estimate=pl.CostEstimate(flops=1 << 16, bytes_accessed=1 << 18, transcendentals=0),
    )(universe, cotangent)


def expand_weights(rank, w1, w2, bias1, bias2, owners, accumulated):
    return pl.pallas_call(
        weights_kernel,
        out_shape=(
            jax.ShapeDtypeStruct((256, 256), BF16),
            jax.ShapeDtypeStruct((256, 768), BF16),
            jax.ShapeDtypeStruct((128, 1536), BF16),
            jax.ShapeDtypeStruct((512, 768), BF16),
            jax.ShapeDtypeStruct((32, 128), F32),
            jax.ShapeDtypeStruct((64, 128), F32),
            jax.ShapeDtypeStruct((1, NB_PAD), jnp.int32),
            jax.ShapeDtypeStruct(accumulated.shape, F32),
        ),
        in_specs=[pl.BlockSpec(memory_space=pltpu.SMEM)] + [whole()] * 7,
        out_specs=(whole(),) * 8,
        scratch_shapes=[pltpu.VMEM((64, 896), F32)],
        compiler_params=params(),
        cost_estimate=pl.CostEstimate(flops=1 << 26, bytes_accessed=4 << 20, transcendentals=0),
    )(rank, w1, jnp.asarray(tap_selection(), BF16), w2, bias1, bias2, owners, accumulated)


def forward_backward(spans, weights):
    return pl.pallas_call(
        main_kernel,
        out_shape=(
            jax.ShapeDtypeStruct((64, 128), BF16),
            jax.ShapeDtypeStruct((NB_PAD, 128), F32),
        ),
        in_specs=[whole()] * 11,
        out_specs=(whole(),) * 2,
        scratch_shapes=[
            pltpu.VMEM((14 * 96, 128), BF16),
            pltpu.VMEM((6 * 256, 128), BF16),
            pltpu.VMEM((4 * 512, 128), BF16),
            pltpu.VMEM((2 * 256, 512), F32),
            pltpu.VMEM((2 * 256, 512), BF16),
            pltpu.VMEM((64, 128), F32),
        ],
        compiler_params=params(),
        cost_estimate=pl.CostEstimate(flops=1 << 31, bytes_accessed=4 << 20, transcendentals=0),
    )(*spans, *weights, jnp.asarray(np.pad(tap_selection().T, ((0, 0), (0, 20))), F32))


def add_owned(blocks, target, kept, feature):
    return pl.pallas_call(
        owned_kernel,
        out_shape=(
            jax.ShapeDtypeStruct(feature.shape, feature.dtype),
            jax.ShapeDtypeStruct(kept.shape, kept.dtype),
        ),
        in_specs=[whole()] * 4,
        out_specs=(whole(),) * 2,
        compiler_params=params(),
        cost_estimate=pl.CostEstimate(flops=1 << 27, bytes_accessed=1 << 20, transcendentals=0),
    )(blocks, target, kept, feature)


SLAB = ("z_hi", "y", "core")
DP = ("z_lo", "x")
PLANE = ("x", "z_hi", "z_lo")
REST = ("core", "y")


def exchange(rows, axes):
    return lax.all_to_all(rows, axes, 0, 0, tiled=True)


def sum_everywhere(blocks):
    width = blocks.shape[1]
    plane, rest = lax.axis_size(PLANE), lax.axis_size(REST)
    part = exchange(blocks, PLANE).reshape(plane, -1, width).sum(axis=0)
    part = exchange(jnp.tile(part, (rest, 1)), REST).reshape(rest, -1, width).sum(axis=0)
    return exchange(jnp.tile(part, (plane, 1)), PLANE)


def body(
    universe, cotangent, conv1_weight, conv1_bias, conv2_weight, conv2_bias, owners, accumulated
):
    slabs = lax.axis_size(SLAB)
    packed, late, early = pack(universe, cotangent.reshape(64, 128))

    def from_slab(distance, rows):
        pairs = [(i, (i - distance) % slabs) for i in range(slabs)]
        return lax.ppermute(rows, SLAB, pairs)

    spans = (from_slab(-1, late), packed, from_slab(1, packed), from_slab(2, early))
    *weights, target, kept = expand_weights(
        lax.axis_index(DP).reshape(1),
        conv1_weight,
        conv2_weight,
        conv1_bias.reshape(1, 32),
        conv2_bias.reshape(1, 64),
        owners.reshape(1, NB),
        accumulated,
    )
    feature, blocks = forward_backward(spans, weights)
    feature, owned = add_owned(sum_everywhere(blocks), target, kept, feature)
    return (feature.reshape(1, 64, 1, 1, 128), owned)


def split_mesh(mesh):
    slabs, ranks = mesh.devices.shape
    x = min(4, ranks)
    y = min(8, slabs // 2)
    shape = (slabs // (2 * y), y, 2, ranks // x, x)
    return Mesh(mesh.devices.reshape(shape), SLAB + DP)


def solution(mesh):
    in_specs = (
        P(DP, None, SLAB, None, None),
        P(DP, None, SLAB, None, None),
        P(),
        P(),
        P(),
        P(),
        P(),
        P(DP, None),
    )
    out_specs = (P(DP, None, SLAB, None, None), P(DP, None))
    return jax.shard_map(
        body, mesh=split_mesh(mesh), in_specs=in_specs, out_specs=out_specs, check_vma=False
    )
```

```python
import jax
import jax.numpy as jnp
import numpy as np
from jax import lax
from jax.experimental import pallas as pl
from jax.experimental.pallas import tpu as pltpu
from jax.sharding import Mesh
from jax.sharding import PartitionSpec as P

NB = 460
NB_PAD = 512
SLOPE = 0.3
BF16 = jnp.bfloat16
F32 = jnp.float32
VMEM_LIMIT = 48 * 1024 * 1024


def tap_selection():
    select = np.zeros((108, 256), np.float32)
    for first in range(3):
        for second in range(3):
            for third in range(3):
                for chan in range(4):
                    lane = (first % 2 * 64 + third * 16 + chan * 4 + second - 1) % 128
                    row = (9 * first + 3 * second + third) * 4 + chan
                    select[row, first // 2 * 128 + lane] = 1.0
    return select


def dot(left, right, precision=None):
    return jnp.dot(left, right, preferred_element_type=F32, precision=precision)


def dot_lanes(left, right):
    return lax.dot_general(left, right, (((1,), (1,)), ((), ())), preferred_element_type=F32)


def lanes_of(shape):
    return lax.broadcasted_iota(jnp.int32, shape, 1)


def turned(value, shift):
    shift = shift % 128
    return pltpu.roll(value, shift, 1) if shift else value


def from_left(value):
    return jnp.where(lanes_of(value.shape) == 0, 0.0, pltpu.roll(value, 1, 1))


def from_right(value):
    return jnp.where(lanes_of(value.shape) == 127, 0.0, pltpu.roll(value, 127, 1))


def side_by_side(ref, at, step, rows):
    return jnp.concatenate([ref[at : at + rows, :], ref[at + step : at + step + rows, :]], axis=1)


def leaky_relu(value):
    return jnp.where(value > 0, value, SLOPE * value)


def slope_mask(value):
    return jnp.where(value > 0, 1.0, SLOPE)


def channel_order():
    row = lax.broadcasted_iota(jnp.int32, (64, 64), 0)
    return jnp.where(lanes_of((64, 64)) == 4 * (row % 16) + row // 16, 1.0, 0.0)


def pack_kernel(
    universe_hbm, cotangent_hbm, own_ref, late_ref, early_ref, universe_ref, cotangent_ref, sems
):
    first = pltpu.make_async_copy(universe_hbm, universe_ref, sems.at[0])
    second = pltpu.make_async_copy(cotangent_hbm, cotangent_ref, sems.at[1])
    first.start()
    second.start()
    first.wait()
    for deep in range(4):
        rows = jnp.concatenate(
            [universe_ref[0, chan, deep].astype(F32) for chan in range(4)], axis=0
        ).astype(BF16)
        own_ref[deep * 16 : deep * 16 + 16, :] = rows
        if deep > 0:
            late_ref[deep * 16 - 16 : deep * 16, :] = rows
        if deep < 3:
            early_ref[deep * 16 : deep * 16 + 16, :] = rows
    second.wait()
    for group in range(4):
        own_ref[64:80, group * 128 : group * 128 + 128] = cotangent_ref[
            group * 16 : group * 16 + 16, :
        ]


def weights_kernel(
    rank_ref,
    w1_hbm,
    w2_hbm,
    bias1_hbm,
    bias2_hbm,
    owners_hbm,
    accumulated_hbm,
    big1_ref,
    big2_ref,
    back_ref,
    comb_ref,
    wide1_ref,
    wide2_ref,
    target_ref,
    kept_ref,
    ordered_ref,
    w1_ref,
    w2_ref,
    bias1_ref,
    bias2_ref,
    owners_ref,
    sems,
):
    pairs = (
        (w2_hbm, w2_ref),
        (w1_hbm, w1_ref),
        (bias1_hbm, bias1_ref),
        (bias2_hbm, bias2_ref),
        (owners_hbm, owners_ref),
        (accumulated_hbm, kept_ref),
    )
    copies = [pltpu.make_async_copy(*pair, sems.at[i]) for i, pair in enumerate(pairs)]
    for copy in copies:
        copy.start()
    for col in range(6):
        cell = lax.broadcasted_iota(jnp.int32, (512, 128), 0)
        comb_ref[:, col * 128 : col * 128 + 128] = jnp.where(
            cell == 4 * lanes_of((512, 128)) + col - 1, 1.0, 0.0
        ).astype(BF16)
    for copy in copies:
        copy.wait()
    ordered_ref[:, 768:896] = jnp.zeros((64, 128), F32)
    ordered_ref[:, 0:864] = dot(channel_order().astype(BF16), w2_ref[...])
    place = lax.broadcasted_iota(jnp.int32, (32, 32), 0) == lanes_of((32, 32))
    column = jnp.sum(jnp.where(place, bias1_ref[...], 0.0), axis=1, keepdims=True)
    wide1_ref[...] = jnp.broadcast_to(column, (32, 128))
    column = jnp.sum(channel_order() * bias2_ref[...], axis=1, keepdims=True)
    wide2_ref[...] = jnp.broadcast_to(column, (64, 128))

    mine = owners_ref[...] == rank_ref[0]
    member = jnp.broadcast_to(jnp.where(mine, 1.0, 0.0), (8, NB)).astype(BF16)
    earlier = lax.broadcasted_iota(jnp.int32, (NB, NB), 0) < lanes_of((NB, NB))
    before = dot(member, jnp.where(earlier, 1.0, 0.0).astype(BF16))[0:1, :]
    target_ref[:, 384:NB_PAD] = jnp.full((1, 128), -1, jnp.int32)
    target_ref[:, 0:NB] = jnp.where(mine, before.astype(jnp.int32), -1)

    q = lax.broadcasted_iota(jnp.int32, (108, 256), 0)
    tap, chan = q >> 2, q & 3
    first = (tap >= 9).astype(jnp.int32) + (tap >= 18).astype(jnp.int32)
    tap = tap - 9 * first
    second = (tap >= 3).astype(jnp.int32) + (tap >= 6).astype(jnp.int32)
    lane = (first & 1) * 64 + (tap - 3 * second) * 16 + chan * 4 + second - 1
    lane = (first >> 1) * 128 + (lane & 127)
    select = jnp.where(lane == lanes_of((108, 256)), 1.0, 0.0).astype(BF16)
    base = dot(w1_ref[...], select)
    y_of = lanes_of((32, 128)) % 4
    for y in range(4):
        near = jnp.abs(y_of - y) <= 1
        for r in range(2):
            for at in (0, 128):
                part = turned(base[:, at : at + 128], r * 16 + y)
                big1_ref[(y * 2 + r) * 32 : (y * 2 + r) * 32 + 32, at : at + 128] = jnp.where(
                    near, part, 0.0
                ).astype(BF16)
    group = lanes_of((64, 128)) // 32

    def gathered(taps):
        result = jnp.zeros((64, 128), F32)
        for place, tap in enumerate(taps):
            if tap is not None:
                column = ordered_ref[:, tap // 4 * 128 : tap // 4 * 128 + 128]
                result = jnp.where(group == place, turned(column, (place - tap) * 32), result)
        return result

    for first in range(3):
        for second in range(3):
            for ph in range(2):
                taps = [
                    (first * 3 + second) * 3 + col - ph if 0 <= col - ph <= 2 else None
                    for col in range(4)
                ]
                tile = gathered(taps).astype(BF16)
                for y in range(2):
                    other = y + second - 1
                    if 0 <= other < 2:
                        big2_ref[
                            (y * 2 + ph) * 64 : (y * 2 + ph) * 64 + 64,
                            first * 256 + other * 128 : first * 256 + other * 128 + 128,
                        ] = tile
    for first in range(3):
        for other in range(2):
            for pair in range(2):
                tiles = []
                for col in (2 * pair, 2 * pair + 1):
                    taps = [
                        ((2 - first) * 3 + 1 - (other - y)) * 3 + 2 - (col - ph)
                        if 0 <= col - ph <= 2
                        else None
                        for y in range(2)
                        for ph in range(2)
                    ]
                    tiles.append(gathered(taps))
                at = first * 512 + other * 256 + pair * 128
                back_ref[:, at : at + 128] = jnp.concatenate(tiles, axis=0).T.astype(BF16)


def main_kernel(
    prev_ref,
    own_ref,
    next_ref,
    after_ref,
    big1_ref,
    big2_ref,
    back_ref,
    comb_ref,
    wide1_ref,
    wide2_ref,
    select_ref,
    feature_ref,
    blocks_ref,
    field_ref,
    pooled_ref,
    delta2_ref,
    pre_ref,
    delta1_ref,
    order_ref,
):
    source = jnp.concatenate(
        [prev_ref[...], own_ref[0:64, :], next_ref[0:64, :], after_ref[...]], axis=0
    )
    for col in range(6):
        part = dot(source, comb_ref[:, col * 128 : col * 128 + 128]).astype(BF16)
        for layer in range(14):
            at = layer * 96 + col * 16
            field_ref[at : at + 16, :] = part[layer * 16 : layer * 16 + 16, :]
    empty = jnp.zeros((64, 128), BF16)

    def around(half):
        parts = []
        for deep in range(2):
            for pair in range(2):
                at = (2 * half + deep) * 96 + pair * 32
                layers = [field_ref[at + first * 96 : at + first * 96 + 64, :] for first in range(3)]
                parts.append(jnp.concatenate(layers + [empty], axis=0))
        return jnp.concatenate(parts, axis=1)

    bias1 = wide1_ref[...]
    for half in range(6):
        conv = dot(big1_ref[...], around(half))
        for y in range(2):
            means = []
            for pair in range(2):
                total = None
                for deep in range(2):
                    lane = (deep * 2 + pair) * 128
                    for row in range(y * 128, y * 128 + 128, 32):
                        block = conv[row : row + 32, lane : lane + 128] + bias1
                        if half in (2, 3):
                            at = (half - 2) * 256 + row
                            pre_ref[at : at + 32, lane : lane + 128] = block
                        value = leaky_relu(block)
                        total = value if total is None else total + value
                means.append((total * 0.125).astype(BF16).astype(F32))
            even, odd = means
            at = half * 256 + y * 128
            pooled_ref[at : at + 128, :] = jnp.concatenate(
                [from_left(odd), even, odd, from_right(even)], axis=0
            ).astype(BF16)

    bias2 = wide2_ref[...]
    total = jnp.zeros((64, 128), F32)
    plain = jnp.concatenate(
        [
            jnp.concatenate([ref[64:80, g * 128 : g * 128 + 128] for g in range(4)], axis=0)
            for ref in (own_ref, next_ref)
        ],
        axis=1,
    )
    upstreams = dot(channel_order().astype(BF16), plain) * 0.125
    for half in range(4):
        if half % 2 == 0:
            conv = dot(big2_ref[...], side_by_side(pooled_ref, half * 256, 256, 768))
        lane = half % 2 * 128
        upstream = upstreams[:, half // 2 * 128 : half // 2 * 128 + 128]
        for y in range(2):
            deltas = []
            for ph in range(2):
                row = (y * 2 + ph) * 64
                block = conv[row : row + 64, lane : lane + 128] + bias2
                if half < 2:
                    total = total + leaky_relu(block)
                deltas.append((upstream * slope_mask(block)).astype(BF16).astype(F32))
            at = half * 512 + y * 256
            delta2_ref[at : at + 256, :] = jnp.concatenate(
                [from_left(deltas[1]), deltas[0], deltas[1], from_right(deltas[0])], axis=0
            ).astype(BF16)
    feature = total * 0.125
    for u in range(4):
        order_ref[pl.ds(u, 16, stride=4), :] = feature[u * 16 : u * 16 + 16, :]
    feature_ref[...] = order_ref[...].astype(BF16)

    ones = jnp.ones((8, 256), BF16)
    delta = jnp.concatenate(
        [side_by_side(delta2_ref, 512 + y * 256 + 64, 512, 128) for y in range(2)], axis=0
    )
    grad2 = dot_lanes(delta, side_by_side(pooled_ref, 256, 256, 768))
    bias_sum2 = dot_lanes(ones, delta)

    backs = dot(back_ref[...], side_by_side(delta2_ref, 0, 512, 1536)) * 0.125
    ones = jnp.ones((8, 512), BF16)
    grad1 = None
    bias_sum1 = None
    for half in range(2):
        for deep in range(2):
            for pair in range(2):
                lane = (deep * 2 + pair) * 128
                for row in range(0, 256, 32):
                    slot = (row // 128 * 2 + pair) * 32
                    back = backs[slot : slot + 32, half * 128 : half * 128 + 128]
                    at = half * 256 + row
                    delta1_ref[at : at + 32, lane : lane + 128] = (
                        back * slope_mask(pre_ref[at : at + 32, lane : lane + 128])
                    ).astype(BF16)
        delta = delta1_ref[half * 256 : half * 256 + 256, :]
        term = dot_lanes(delta, around(half + 2))
        bias_term = dot_lanes(ones, delta)
        grad1 = term if grad1 is None else grad1 + term
        bias_sum1 = bias_term if bias_sum1 is None else bias_sum1 + bias_term

    exact = lax.Precision.HIGHEST
    bias_row1 = bias_sum1[:, 0:128] + bias_sum1[:, 128:256]
    bias_row1 = bias_row1 + turned(bias_row1, 64)
    bias_row1 = bias_row1 + turned(bias_row1, 32)
    q = lax.broadcasted_iota(jnp.int32, (128, 128), 0)
    lane = 32 + 4 * (q % 16) + q % 64 // 16
    bias_row2 = dot(
        bias_sum2[:, 0:128] + bias_sum2[:, 128:256],
        jnp.where(lane == lanes_of((128, 128)), 1.0, 0.0),
        exact,
    )

    y_of = lanes_of((32, 128)) % 4
    parts = []
    for at in (0, 128):
        part = jnp.zeros((32, 128), F32)
        for y in range(4):
            near = jnp.abs(y_of - y) <= 1
            for r in range(2):
                row = (y * 2 + r) * 32
                block = grad1[row : row + 32, at : at + 128]
                part = part + turned(jnp.where(near, block, 0.0), -(r * 16 + y))
        parts.append(part)
    flat1 = dot(jnp.concatenate(parts, axis=1), select_ref[...], exact)
    rows = [None] * 28
    lane8 = lanes_of((8, 128))
    for o in range(32):
        begin = o * 108 // 128
        shift = o * 108 % 128
        moved = turned(flat1[o // 8 * 8 : o // 8 * 8 + 8, :], shift)
        for row, kept in ((begin, lane8 >= shift), (begin + 1, lane8 < shift)):
            if row == begin or shift + 108 > 128:
                term = jnp.where(kept, moved, 0.0)[o % 8 : o % 8 + 1, :]
                rows[row] = term if rows[row] is None else rows[row] + term
    for row in range(27):
        blocks_ref[row : row + 1, :] = rows[row]

    taps = []
    for first in range(3):
        for second in range(3):
            part = None
            for y in range(2):
                other = y + second - 1
                if 0 <= other < 2:
                    for ph in range(2):
                        row = (y * 2 + ph) * 64
                        at = first * 256 + other * 128
                        block = turned(grad2[row : row + 64, at : at + 128], -ph * 32)
                        part = block if part is None else part + block
            taps.append(part)
    group = lanes_of((16, 128)) // 32

    def chunk(number, place):
        u, tap = (number - 1) // 27, (number - 1) % 27
        return turned(taps[tap // 3][u * 16 : u * 16 + 16, :], (place - tap % 3) * 32)

    last = pltpu.roll(chunk(108, 0), 1, 0)
    row_of = lax.broadcasted_iota(jnp.int32, (16, 128), 0)
    for k in range(27):
        if k == 0:
            value = jnp.where(row_of == 0, jnp.broadcast_to(bias_row1[0:1, :], (16, 128)), last)
        else:
            value = chunk(4 * k, 0)
        for place in range(1, 4):
            value = jnp.where(group == place, chunk(4 * k + place, place), value)
        blocks_ref[pl.ds(27 + k, 16, stride=27), :] = value
    blocks_ref[459:460, :] = jnp.where(lanes_of((1, 128)) < 32, last[0:1, :], bias_row2[0:1, :])
    blocks_ref[NB:NB_PAD, :] = jnp.zeros((NB_PAD - NB, 128), F32)


def owned_kernel(blocks_ref, target_ref, kept_ref, feature_ref, feature_out_ref, owned_ref):
    feature_out_ref[...] = feature_ref[...]
    capacity = owned_ref.shape[0]
    rows = -(-capacity // 16) * 16
    blocks = blocks_ref[...]
    high = blocks.astype(BF16)
    rest = blocks - high.astype(F32)
    middle = rest.astype(BF16)
    low = (rest - middle.astype(F32)).astype(BF16)
    row_at = lax.broadcasted_iota(jnp.int32, (rows, NB_PAD), 0)
    placing = jnp.where(row_at == target_ref[...], 1.0, 0.0).astype(BF16)
    moved = dot(placing, jnp.concatenate([high, middle, low], axis=1))
    total = moved[:, 0:128] + moved[:, 128:256] + moved[:, 256:384]
    owned_ref[...] = kept_ref[...] + total[0:capacity, :]


def whole():
    return pl.BlockSpec(memory_space=pltpu.VMEM)


def params():
    return pltpu.CompilerParams(vmem_limit_bytes=VMEM_LIMIT)


def pack(universe, cotangent):
    return pl.pallas_call(
        pack_kernel,
        out_shape=(
            jax.ShapeDtypeStruct((80, 512), BF16),
            jax.ShapeDtypeStruct((48, 512), BF16),
            jax.ShapeDtypeStruct((48, 512), BF16),
        ),
        in_specs=[pl.BlockSpec(memory_space=pltpu.HBM)] * 2,
        out_specs=(whole(),) * 3,
        scratch_shapes=[
            pltpu.VMEM(universe.shape, BF16),
            pltpu.VMEM(cotangent.shape, BF16),
            pltpu.SemaphoreType.DMA((2,)),
        ],
        compiler_params=params(),
        cost_estimate=pl.CostEstimate(flops=1 << 16, bytes_accessed=1 << 18, transcendentals=0),
    )(*(pltpu.with_memory_space_constraint(x, pltpu.HBM) for x in (universe, cotangent)))


def expand_weights(rank, w1, w2, bias1, bias2, owners, accumulated):
    return pl.pallas_call(
        weights_kernel,
        out_shape=(
            jax.ShapeDtypeStruct((256, 256), BF16),
            jax.ShapeDtypeStruct((256, 768), BF16),
            jax.ShapeDtypeStruct((128, 1536), BF16),
            jax.ShapeDtypeStruct((512, 768), BF16),
            jax.ShapeDtypeStruct((32, 128), F32),
            jax.ShapeDtypeStruct((64, 128), F32),
            jax.ShapeDtypeStruct((1, NB_PAD), jnp.int32),
            jax.ShapeDtypeStruct(accumulated.shape, F32),
        ),
        in_specs=[pl.BlockSpec(memory_space=pltpu.SMEM)] + [pl.BlockSpec(memory_space=pltpu.HBM)] * 6,
        out_specs=(whole(),) * 8,
        scratch_shapes=[
            pltpu.VMEM((64, 896), F32),
            pltpu.VMEM((32, 108), BF16),
            pltpu.VMEM((64, 864), BF16),
            pltpu.VMEM((1, 32), F32),
            pltpu.VMEM((1, 64), F32),
            pltpu.VMEM((1, NB), jnp.int32),
            pltpu.SemaphoreType.DMA((6,)),
        ],
        compiler_params=params(),
        cost_estimate=pl.CostEstimate(flops=1 << 26, bytes_accessed=4 << 20, transcendentals=0),
    )(rank, *(pltpu.with_memory_space_constraint(x, pltpu.HBM) for x in (w1, w2, bias1, bias2, owners, accumulated)))


def forward_backward(spans, weights):
    return pl.pallas_call(
        main_kernel,
        out_shape=(
            jax.ShapeDtypeStruct((64, 128), BF16),
            jax.ShapeDtypeStruct((NB_PAD, 128), F32),
        ),
        in_specs=[whole()] * 11,
        out_specs=(whole(),) * 2,
        scratch_shapes=[
            pltpu.VMEM((14 * 96, 128), BF16),
            pltpu.VMEM((6 * 256, 128), BF16),
            pltpu.VMEM((4 * 512, 128), BF16),
            pltpu.VMEM((2 * 256, 512), F32),
            pltpu.VMEM((2 * 256, 512), BF16),
            pltpu.VMEM((64, 128), F32),
        ],
        compiler_params=params(),
        cost_estimate=pl.CostEstimate(flops=1 << 31, bytes_accessed=4 << 20, transcendentals=0),
    )(*spans, *weights, jnp.asarray(np.pad(tap_selection().T, ((0, 0), (0, 20))), F32))


def add_owned(blocks, target, kept, feature):
    return pl.pallas_call(
        owned_kernel,
        out_shape=(
            jax.ShapeDtypeStruct(feature.shape, feature.dtype),
            jax.ShapeDtypeStruct(kept.shape, kept.dtype),
        ),
        in_specs=[whole()] * 4,
        out_specs=(whole(),) * 2,
        compiler_params=params(),
        cost_estimate=pl.CostEstimate(flops=1 << 27, bytes_accessed=1 << 20, transcendentals=0),
    )(blocks, target, kept, feature)


SLAB = ("z_hi", "y", "core")
DP = ("z_lo", "x")
PLANE = ("x", "z_hi", "z_lo")
REST = ("core", "y")


def exchange(rows, axes):
    return lax.all_to_all(rows, axes, 0, 0, tiled=True)


def sum_everywhere(blocks):
    width = blocks.shape[1]
    plane, rest = lax.axis_size(PLANE), lax.axis_size(REST)
    part = exchange(blocks, PLANE).reshape(plane, -1, width).sum(axis=0)
    part = exchange(jnp.tile(part, (rest, 1)), REST).reshape(rest, -1, width).sum(axis=0)
    return exchange(jnp.tile(part, (plane, 1)), PLANE)


def body(
    universe, cotangent, conv1_weight, conv1_bias, conv2_weight, conv2_bias, owners, accumulated
):
    slabs = lax.axis_size(SLAB)
    packed, late, early = pack(universe, cotangent.reshape(64, 128))

    def from_slab(distance, rows):
        pairs = [(i, (i - distance) % slabs) for i in range(slabs)]
        return lax.ppermute(rows, SLAB, pairs)

    spans = (from_slab(-1, late), packed, from_slab(1, packed), from_slab(2, early))
    *weights, target, kept = expand_weights(
        lax.axis_index(DP).reshape(1),
        conv1_weight,
        conv2_weight,
        conv1_bias.reshape(1, 32),
        conv2_bias.reshape(1, 64),
        owners.reshape(1, NB),
        accumulated,
    )
    feature, blocks = forward_backward(spans, weights)
    feature, owned = add_owned(sum_everywhere(blocks), target, kept, feature)
    return (feature.reshape(1, 64, 1, 1, 128), owned)


def split_mesh(mesh):
    slabs, ranks = mesh.devices.shape
    x = min(4, ranks)
    y = min(8, slabs // 2)
    shape = (slabs // (2 * y), y, 2, ranks // x, x)
    return Mesh(mesh.devices.reshape(shape), SLAB + DP)


def solution(mesh):
    in_specs = (
        P(DP, None, SLAB, None, None),
        P(DP, None, SLAB, None, None),
        P(),
        P(),
        P(),
        P(),
        P(),
        P(DP, None),
    )
    out_specs = (P(DP, None, SLAB, None, None), P(DP, None))
    return jax.shard_map(
        body, mesh=split_mesh(mesh), in_specs=in_specs, out_specs=out_specs, check_vma=False
    )
```

```python
import jax
import jax.numpy as jnp
import numpy as np
from jax import lax
from jax.experimental import pallas as pl
from jax.experimental.pallas import tpu as pltpu
from jax.sharding import Mesh
from jax.sharding import PartitionSpec as P

NB = 460
NB_PAD = 512
SLOPE = 0.3
BF16 = jnp.bfloat16
F32 = jnp.float32
VMEM_LIMIT = 48 * 1024 * 1024


def tap_selection():
    select = np.zeros((108, 256), np.float32)
    for first in range(3):
        for second in range(3):
            for third in range(3):
                for chan in range(4):
                    lane = (first % 2 * 64 + third * 16 + chan * 4 + second - 1) % 128
                    row = (9 * first + 3 * second + third) * 4 + chan
                    select[row, first // 2 * 128 + lane] = 1.0
    return select


def dot(left, right, precision=None):
    return jnp.dot(left, right, preferred_element_type=F32, precision=precision)


def dot_lanes(left, right):
    return lax.dot_general(left, right, (((1,), (1,)), ((), ())), preferred_element_type=F32)


def lanes_of(shape):
    return lax.broadcasted_iota(jnp.int32, shape, 1)


def turned(value, shift):
    shift = shift % 128
    return pltpu.roll(value, shift, 1) if shift else value


def from_left(value):
    return jnp.where(lanes_of(value.shape) == 0, 0.0, pltpu.roll(value, 1, 1))


def from_right(value):
    return jnp.where(lanes_of(value.shape) == 127, 0.0, pltpu.roll(value, 127, 1))


def leaky_relu(value):
    return jnp.where(value > 0, value, SLOPE * value)


def slope_mask(value):
    return jnp.where(value > 0, 1.0, SLOPE)


def channel_order():
    row = lax.broadcasted_iota(jnp.int32, (64, 64), 0)
    return jnp.where(lanes_of((64, 64)) == 4 * (row % 16) + row // 16, 1.0, 0.0)


def pack_kernel(
    universe_hbm,
    cotangent_hbm,
    w1_hbm,
    w2_hbm,
    bias1_hbm,
    bias2_hbm,
    owners_hbm,
    accumulated_hbm,
    own_ref,
    late_ref,
    early_ref,
    w1_ref,
    w2_ref,
    bias1_ref,
    bias2_ref,
    owners_ref,
    kept_ref,
    universe_ref,
    cotangent_ref,
    sems,
):
    first = pltpu.make_async_copy(universe_hbm, universe_ref, sems.at[0])
    second = pltpu.make_async_copy(cotangent_hbm, cotangent_ref, sems.at[1])
    first.start()
    second.start()
    pairs = (
        (w1_hbm, w1_ref),
        (w2_hbm, w2_ref),
        (bias1_hbm, bias1_ref),
        (bias2_hbm, bias2_ref),
        (owners_hbm, owners_ref),
        (accumulated_hbm, kept_ref),
    )
    others = [pltpu.make_async_copy(*pair, sems.at[i + 2]) for i, pair in enumerate(pairs)]
    for copy in others:
        copy.start()
    first.wait()
    for deep in range(4):
        rows = jnp.concatenate(
            [universe_ref[0, chan, deep].astype(F32) for chan in range(4)], axis=0
        ).astype(BF16)
        own_ref[deep * 16 : deep * 16 + 16, :] = rows
        if deep > 0:
            late_ref[deep * 16 - 16 : deep * 16, :] = rows
        early_ref[deep * 16 : deep * 16 + 16, :] = rows
    second.wait()
    for group in range(4):
        own_ref[64:80, group * 128 : group * 128 + 128] = cotangent_ref[
            group * 16 : group * 16 + 16, :
        ]
    for copy in others:
        copy.wait()


def weights_kernel(
    rank_ref,
    w1_ref,
    w2_ref,
    bias1_ref,
    bias2_ref,
    owners_ref,
    big1_ref,
    big2_ref,
    back_ref,
    comb_ref,
    wide1_ref,
    wide2_ref,
    target_ref,
    ordered_ref,
):
    for col in range(6):
        cell = lax.broadcasted_iota(jnp.int32, (512, 128), 0)
        comb_ref[:, col * 128 : col * 128 + 128] = jnp.where(
            cell == 4 * lanes_of((512, 128)) + col - 1, 1.0, 0.0
        ).astype(BF16)
    ordered_ref[:, 768:896] = jnp.zeros((64, 128), F32)
    ordered_ref[:, 0:864] = dot(channel_order().astype(BF16), w2_ref[...])
    place = lax.broadcasted_iota(jnp.int32, (32, 32), 0) == lanes_of((32, 32))
    column = jnp.sum(jnp.where(place, bias1_ref[...], 0.0), axis=1, keepdims=True)
    wide1_ref[...] = jnp.broadcast_to(column, (32, 128))
    column = jnp.sum(channel_order() * bias2_ref[...], axis=1, keepdims=True)
    wide2_ref[...] = jnp.broadcast_to(column, (64, 128))

    mine = owners_ref[...] == rank_ref[0]
    member = jnp.broadcast_to(jnp.where(mine, 1.0, 0.0), (8, NB)).astype(BF16)
    earlier = lax.broadcasted_iota(jnp.int32, (NB, NB), 0) < lanes_of((NB, NB))
    before = dot(member, jnp.where(earlier, 1.0, 0.0).astype(BF16))[0:1, :]
    target_ref[:, 384:NB_PAD] = jnp.full((1, 128), -1, jnp.int32)
    target_ref[:, 0:NB] = jnp.where(mine, before.astype(jnp.int32), -1)

    q = lax.broadcasted_iota(jnp.int32, (108, 256), 0)
    tap, chan = q >> 2, q & 3
    first = (tap >= 9).astype(jnp.int32) + (tap >= 18).astype(jnp.int32)
    tap = tap - 9 * first
    second = (tap >= 3).astype(jnp.int32) + (tap >= 6).astype(jnp.int32)
    lane = (first & 1) * 64 + (tap - 3 * second) * 16 + chan * 4 + second - 1
    lane = (first >> 1) * 128 + (lane & 127)
    select = jnp.where(lane == lanes_of((108, 256)), 1.0, 0.0).astype(BF16)
    base = dot(w1_ref[...], select)
    y_of = lanes_of((32, 128)) % 4
    for y in range(4):
        near = jnp.abs(y_of - y) <= 1
        for r in range(2):
            for at in (0, 128):
                part = turned(base[:, at : at + 128], r * 16 + y)
                big1_ref[(y * 2 + r) * 32 : (y * 2 + r) * 32 + 32, at : at + 128] = jnp.where(
                    near, part, 0.0
                ).astype(BF16)
    group = lanes_of((64, 128)) // 32

    def gathered(taps):
        result = jnp.zeros((64, 128), F32)
        for place, tap in enumerate(taps):
            if tap is not None:
                column = ordered_ref[:, tap // 4 * 128 : tap // 4 * 128 + 128]
                result = jnp.where(group == place, turned(column, (place - tap) * 32), result)
        return result

    for first in range(3):
        for second in range(3):
            for ph in range(2):
                taps = [
                    (first * 3 + second) * 3 + col - ph if 0 <= col - ph <= 2 else None
                    for col in range(4)
                ]
                tile = gathered(taps).astype(BF16)
                for y in range(2):
                    other = y + second - 1
                    if 0 <= other < 2:
                        big2_ref[
                            (y * 2 + ph) * 64 : (y * 2 + ph) * 64 + 64,
                            first * 256 + other * 128 : first * 256 + other * 128 + 128,
                        ] = tile
    for first in range(3):
        for other in range(2):
            for pair in range(2):
                tiles = []
                for col in (2 * pair, 2 * pair + 1):
                    taps = [
                        ((2 - first) * 3 + 1 - (other - y)) * 3 + 2 - (col - ph)
                        if 0 <= col - ph <= 2
                        else None
                        for y in range(2)
                        for ph in range(2)
                    ]
                    tiles.append(gathered(taps))
                at = first * 512 + other * 256 + pair * 128
                back_ref[:, at : at + 128] = jnp.concatenate(tiles, axis=0).T.astype(BF16)


def expand(source, comb_ref, field_ref):
    for col in range(6):
        part = dot(source, comb_ref[:, col * 128 : col * 128 + 128]).astype(BF16)
        for layer in range(source.shape[0] // 16):
            at = layer * 96 + col * 16
            field_ref[at : at + 16, :] = part[layer * 16 : layer * 16 + 16, :]


def around(layers, half):
    empty = jnp.zeros((64, 128), BF16)
    parts = []
    for deep in range(2):
        for pair in range(2):
            pieces = []
            for first in range(3):
                ref, at = layers(2 * half + deep + first)
                pieces.append(ref[at + pair * 32 : at + pair * 32 + 64, :])
            parts.append(jnp.concatenate(pieces + [empty], axis=0))
    return jnp.concatenate(parts, axis=1)


def stacks(pieces, begin):
    columns = [
        jnp.concatenate([pieces(half) for half in range(at, at + 3)], axis=0)
        for at in (begin, begin + 1)
    ]
    return jnp.concatenate(columns, axis=1)


def pool_first(conv, bias1, pooled_ref, at, pre_ref, pre_at):
    for y in range(2):
        means = []
        for pair in range(2):
            total = None
            for deep in range(2):
                lane = (deep * 2 + pair) * 128
                for row in range(y * 128, y * 128 + 128, 32):
                    block = conv[row : row + 32, lane : lane + 128] + bias1
                    if pre_ref is not None:
                        pre_ref[pre_at + row : pre_at + row + 32, lane : lane + 128] = block
                    value = leaky_relu(block)
                    total = value if total is None else total + value
            means.append((total * 0.125).astype(BF16).astype(F32))
        even, odd = means
        pooled_ref[at + y * 128 : at + y * 128 + 128, :] = jnp.concatenate(
            [from_left(odd), even, odd, from_right(even)], axis=0
        ).astype(BF16)


def delta_second(conv, bias2, cotangent_ref, delta2_ref):
    plain = [cotangent_ref[64:80, g * 128 : g * 128 + 128] for g in range(4)]
    upstream = dot(channel_order().astype(BF16), jnp.concatenate(plain, axis=0)) * 0.125
    total = jnp.zeros((64, 128), F32)
    for half in range(2):
        lane = half * 128
        for y in range(2):
            deltas = []
            for ph in range(2):
                row = (y * 2 + ph) * 64
                block = conv[row : row + 64, lane : lane + 128] + bias2
                total = total + leaky_relu(block)
                deltas.append((upstream * slope_mask(block)).astype(BF16).astype(F32))
            at = half * 512 + y * 256
            delta2_ref[at : at + 256, :] = jnp.concatenate(
                [from_left(deltas[1]), deltas[0], deltas[1], from_right(deltas[0])], axis=0
            ).astype(BF16)
    return total


def late_kernel(
    own_ref,
    next_ref,
    after_ref,
    big1_ref,
    big2_ref,
    comb_ref,
    wide1_ref,
    wide2_ref,
    field_ref,
    pooled_ref,
    pre_ref,
    delta2_ref,
):
    source = jnp.concatenate(
        [own_ref[0:64, :], next_ref[0:64, :], after_ref[0:48, :]], axis=0
    )
    expand(source, comb_ref, field_ref)

    def layers(layer):
        return field_ref, (layer - 3) * 96

    for half in range(2, 6):
        conv = dot(big1_ref[...], around(layers, half))
        kept = pre_ref if half < 4 else None
        pool_first(conv, wide1_ref[...], pooled_ref, (half - 2) * 256, kept, (half - 2) * 256)

    def pooled(half):
        return pooled_ref[(half - 2) * 256 : (half - 1) * 256, :]

    conv = dot(big2_ref[...], stacks(pooled, 2))
    delta_second(conv, wide2_ref[...], next_ref, delta2_ref)


def main_kernel(
    prev_ref,
    own_ref,
    late_field_ref,
    late_pooled_ref,
    pre_ref,
    late_delta2_ref,
    big1_ref,
    big2_ref,
    back_ref,
    comb_ref,
    wide1_ref,
    wide2_ref,
    select_ref,
    feature_ref,
    blocks_ref,
    field_ref,
    pooled_ref,
    delta2_ref,
    delta1_ref,
    order_ref,
):
    expand(prev_ref[...], comb_ref, field_ref)

    def layers(layer):
        return (field_ref, layer * 96) if layer < 3 else (late_field_ref, (layer - 3) * 96)

    def pooled(half):
        ref, at = (pooled_ref, half * 256) if half < 2 else (late_pooled_ref, (half - 2) * 256)
        return ref[at : at + 256, :]

    def delta_rows(half, begin, rows):
        ref, at = (delta2_ref, half * 512) if half < 2 else (late_delta2_ref, (half - 2) * 512)
        return ref[at + begin : at + begin + rows, :]

    for half in range(2):
        conv = dot(big1_ref[...], around(layers, half))
        pool_first(conv, wide1_ref[...], pooled_ref, half * 256, None, 0)
    conv = dot(big2_ref[...], stacks(pooled, 0))
    feature = delta_second(conv, wide2_ref[...], own_ref, delta2_ref) * 0.125
    for u in range(4):
        order_ref[pl.ds(u, 16, stride=4), :] = feature[u * 16 : u * 16 + 16, :]
    feature_ref[...] = order_ref[...].astype(BF16)

    ones = jnp.ones((8, 256), BF16)
    delta = jnp.concatenate(
        [
            jnp.concatenate([delta_rows(half, y * 256 + 64, 128) for half in (1, 2)], axis=1)
            for y in range(2)
        ],
        axis=0,
    )
    grad2 = dot_lanes(delta, stacks(pooled, 1))
    bias_sum2 = dot_lanes(ones, delta)

    backs = dot(back_ref[...], stacks(lambda half: delta_rows(half, 0, 512), 0)) * 0.125
    ones = jnp.ones((8, 512), BF16)
    grad1 = None
    bias_sum1 = None
    for half in range(2):
        for deep in range(2):
            for pair in range(2):
                lane = (deep * 2 + pair) * 128
                for row in range(0, 256, 32):
                    slot = (row // 128 * 2 + pair) * 32
                    back = backs[slot : slot + 32, half * 128 : half * 128 + 128]
                    at = half * 256 + row
                    delta1_ref[at : at + 32, lane : lane + 128] = (
                        back * slope_mask(pre_ref[at : at + 32, lane : lane + 128])
                    ).astype(BF16)
        delta = delta1_ref[half * 256 : half * 256 + 256, :]
        term = dot_lanes(delta, around(layers, half + 2))
        bias_term = dot_lanes(ones, delta)
        grad1 = term if grad1 is None else grad1 + term
        bias_sum1 = bias_term if bias_sum1 is None else bias_sum1 + bias_term

    exact = lax.Precision.HIGHEST
    bias_row1 = bias_sum1[:, 0:128] + bias_sum1[:, 128:256]
    bias_row1 = bias_row1 + turned(bias_row1, 64)
    bias_row1 = bias_row1 + turned(bias_row1, 32)
    q = lax.broadcasted_iota(jnp.int32, (128, 128), 0)
    lane = 32 + 4 * (q % 16) + q % 64 // 16
    bias_row2 = dot(
        bias_sum2[:, 0:128] + bias_sum2[:, 128:256],
        jnp.where(lane == lanes_of((128, 128)), 1.0, 0.0),
        exact,
    )

    y_of = lanes_of((32, 128)) % 4
    parts = []
    for at in (0, 128):
        part = jnp.zeros((32, 128), F32)
        for y in range(4):
            near = jnp.abs(y_of - y) <= 1
            for r in range(2):
                row = (y * 2 + r) * 32
                block = grad1[row : row + 32, at : at + 128]
                part = part + turned(jnp.where(near, block, 0.0), -(r * 16 + y))
        parts.append(part)
    flat1 = dot(jnp.concatenate(parts, axis=1), select_ref[...], exact)
    rows = [None] * 28
    lane8 = lanes_of((8, 128))
    for o in range(32):
        begin = o * 108 // 128
        shift = o * 108 % 128
        moved = turned(flat1[o // 8 * 8 : o // 8 * 8 + 8, :], shift)
        for row, kept in ((begin, lane8 >= shift), (begin + 1, lane8 < shift)):
            if row == begin or shift + 108 > 128:
                term = jnp.where(kept, moved, 0.0)[o % 8 : o % 8 + 1, :]
                rows[row] = term if rows[row] is None else rows[row] + term
    for row in range(27):
        blocks_ref[row : row + 1, :] = rows[row]

    taps = []
    for first in range(3):
        for second in range(3):
            part = None
            for y in range(2):
                other = y + second - 1
                if 0 <= other < 2:
                    for ph in range(2):
                        row = (y * 2 + ph) * 64
                        at = first * 256 + other * 128
                        block = turned(grad2[row : row + 64, at : at + 128], -ph * 32)
                        part = block if part is None else part + block
            taps.append(part)
    group = lanes_of((16, 128)) // 32

    def chunk(number, place):
        u, tap = (number - 1) // 27, (number - 1) % 27
        return turned(taps[tap // 3][u * 16 : u * 16 + 16, :], (place - tap % 3) * 32)

    last = pltpu.roll(chunk(108, 0), 1, 0)
    row_of = lax.broadcasted_iota(jnp.int32, (16, 128), 0)
    for k in range(27):
        if k == 0:
            value = jnp.where(row_of == 0, jnp.broadcast_to(bias_row1[0:1, :], (16, 128)), last)
        else:
            value = chunk(4 * k, 0)
        for place in range(1, 4):
            value = jnp.where(group == place, chunk(4 * k + place, place), value)
        blocks_ref[pl.ds(27 + k, 16, stride=27), :] = value
    blocks_ref[459:460, :] = jnp.where(lanes_of((1, 128)) < 32, last[0:1, :], bias_row2[0:1, :])
    blocks_ref[NB:NB_PAD, :] = jnp.zeros((NB_PAD - NB, 128), F32)


def owned_kernel(blocks_ref, target_ref, kept_ref, feature_ref, feature_out_ref, owned_ref):
    feature_out_ref[...] = feature_ref[...]
    capacity = owned_ref.shape[0]
    rows = -(-capacity // 16) * 16
    blocks = blocks_ref[...]
    high = blocks.astype(BF16)
    rest = blocks - high.astype(F32)
    middle = rest.astype(BF16)
    low = (rest - middle.astype(F32)).astype(BF16)
    row_at = lax.broadcasted_iota(jnp.int32, (rows, NB_PAD), 0)
    placing = jnp.where(row_at == target_ref[...], 1.0, 0.0).astype(BF16)
    moved = dot(placing, jnp.concatenate([high, middle, low], axis=1))
    total = moved[:, 0:128] + moved[:, 128:256] + moved[:, 256:384]
    owned_ref[...] = kept_ref[...] + total[0:capacity, :]


def whole():
    return pl.BlockSpec(memory_space=pltpu.VMEM)


def params():
    return pltpu.CompilerParams(vmem_limit_bytes=VMEM_LIMIT)


def pack(*operands):
    universe, cotangent, *others = operands
    return pl.pallas_call(
        pack_kernel,
        out_shape=(
            jax.ShapeDtypeStruct((80, 512), BF16),
            jax.ShapeDtypeStruct((48, 512), BF16),
            jax.ShapeDtypeStruct((64, 512), BF16),
            *(jax.ShapeDtypeStruct(x.shape, x.dtype) for x in others),
        ),
        in_specs=[pl.BlockSpec(memory_space=pltpu.HBM)] * 8,
        out_specs=(whole(),) * 9,
        scratch_shapes=[
            pltpu.VMEM(universe.shape, BF16),
            pltpu.VMEM(cotangent.shape, BF16),
            pltpu.SemaphoreType.DMA((8,)),
        ],
        compiler_params=params(),
        cost_estimate=pl.CostEstimate(flops=1 << 16, bytes_accessed=1 << 18, transcendentals=0),
    )(*(pltpu.with_memory_space_constraint(x, pltpu.HBM) for x in operands))


def expand_weights(rank, *operands):
    return pl.pallas_call(
        weights_kernel,
        out_shape=(
            jax.ShapeDtypeStruct((256, 256), BF16),
            jax.ShapeDtypeStruct((256, 768), BF16),
            jax.ShapeDtypeStruct((128, 1536), BF16),
            jax.ShapeDtypeStruct((512, 768), BF16),
            jax.ShapeDtypeStruct((32, 128), F32),
            jax.ShapeDtypeStruct((64, 128), F32),
            jax.ShapeDtypeStruct((1, NB_PAD), jnp.int32),
        ),
        in_specs=[pl.BlockSpec(memory_space=pltpu.SMEM)] + [whole()] * 5,
        out_specs=(whole(),) * 7,
        scratch_shapes=[pltpu.VMEM((64, 896), F32)],
        compiler_params=params(),
        cost_estimate=pl.CostEstimate(flops=1 << 26, bytes_accessed=4 << 20, transcendentals=0),
    )(rank, *operands)


def forward_late(own, following, after, big1, big2, comb, wide1, wide2):
    return pl.pallas_call(
        late_kernel,
        out_shape=(
            jax.ShapeDtypeStruct((11 * 96, 128), BF16),
            jax.ShapeDtypeStruct((4 * 256, 128), BF16),
            jax.ShapeDtypeStruct((2 * 256, 512), F32),
            jax.ShapeDtypeStruct((2 * 512, 128), BF16),
        ),
        in_specs=[whole()] * 8,
        out_specs=(whole(),) * 4,
        compiler_params=params(),
        cost_estimate=pl.CostEstimate(flops=1 << 30, bytes_accessed=4 << 20, transcendentals=0),
    )(own, following, after, big1, big2, comb, wide1, wide2)


def forward_backward(before, own, late, weights):
    return pl.pallas_call(
        main_kernel,
        out_shape=(
            jax.ShapeDtypeStruct((64, 128), BF16),
            jax.ShapeDtypeStruct((NB_PAD, 128), F32),
        ),
        in_specs=[whole()] * 13,
        out_specs=(whole(),) * 2,
        scratch_shapes=[
            pltpu.VMEM((3 * 96, 128), BF16),
            pltpu.VMEM((2 * 256, 128), BF16),
            pltpu.VMEM((2 * 512, 128), BF16),
            pltpu.VMEM((2 * 256, 512), BF16),
            pltpu.VMEM((64, 128), F32),
        ],
        compiler_params=params(),
        cost_estimate=pl.CostEstimate(flops=1 << 30, bytes_accessed=4 << 20, transcendentals=0),
    )(before, own, *late, *weights, jnp.asarray(np.pad(tap_selection().T, ((0, 0), (0, 20))), F32))


def add_owned(blocks, target, kept, feature):
    return pl.pallas_call(
        owned_kernel,
        out_shape=(
            jax.ShapeDtypeStruct(feature.shape, feature.dtype),
            jax.ShapeDtypeStruct(kept.shape, kept.dtype),
        ),
        in_specs=[whole()] * 4,
        out_specs=(whole(),) * 2,
        compiler_params=params(),
        cost_estimate=pl.CostEstimate(flops=1 << 27, bytes_accessed=1 << 20, transcendentals=0),
    )(blocks, target, kept, feature)


SLAB = ("z_hi", "y", "core")
DP = ("z_lo", "x")
PLANE = ("x", "z_lo", "z_hi")
REST = ("core", "y")


def exchange(rows, axes):
    return lax.all_to_all(rows, axes, 0, 0, tiled=True)


def sum_everywhere(blocks):
    width = blocks.shape[1]
    plane, rest = lax.axis_size(PLANE), lax.axis_size(REST)
    part = exchange(blocks, PLANE).reshape(plane, -1, width).sum(axis=0)
    part = exchange(jnp.tile(part, (rest, 1)), REST).reshape(rest, -1, width).sum(axis=0)
    return exchange(jnp.tile(part, (plane, 1)), PLANE)


def body(
    universe, cotangent, conv1_weight, conv1_bias, conv2_weight, conv2_bias, owners, accumulated
):
    slabs = lax.axis_size(SLAB)
    packed, late, early, *others, kept = pack(
        universe,
        cotangent.reshape(64, 128),
        conv1_weight,
        conv2_weight,
        conv1_bias.reshape(1, 32),
        conv2_bias.reshape(1, 64),
        owners.reshape(1, NB),
        accumulated,
    )
    def from_slab(distance, rows):
        pairs = [(i, (i - distance) % slabs) for i in range(slabs)]
        return lax.ppermute(rows, SLAB, pairs)

    before, following, after = from_slab(-1, late), from_slab(1, packed), from_slab(2, early)
    *weights, target = expand_weights(lax.axis_index(DP).reshape(1), *others)
    big1, big2, _, comb, wide1, wide2 = weights
    ahead = forward_late(packed, following, after, big1, big2, comb, wide1, wide2)
    feature, blocks = forward_backward(before, packed, ahead, weights)
    feature, owned = add_owned(sum_everywhere(blocks), target, kept, feature)
    return (feature.reshape(1, 64, 1, 1, 128), owned)


def split_mesh(mesh):
    slabs, ranks = mesh.devices.shape
    x = min(4, ranks)
    y = min(8, slabs // 2)
    shape = (slabs // (2 * y), y, 2, ranks // x, x)
    return Mesh(mesh.devices.reshape(shape), SLAB + DP)


def solution(mesh):
    in_specs = (
        P(DP, None, SLAB, None, None),
        P(DP, None, SLAB, None, None),
        P(),
        P(),
        P(),
        P(),
        P(),
        P(DP, None),
    )
    out_specs = (P(DP, None, SLAB, None, None), P(DP, None))
    return jax.shard_map(
        body, mesh=split_mesh(mesh), in_specs=in_specs, out_specs=out_specs, check_vma=False
    )
```

```python
import jax
import jax.numpy as jnp
import numpy as np
from jax import lax
from jax.experimental import pallas as pl
from jax.experimental.pallas import tpu as pltpu
from jax.sharding import Mesh
from jax.sharding import PartitionSpec as P

NB = 460
NB_PAD = 512
SLOPE = 0.3
BF16 = jnp.bfloat16
F32 = jnp.float32
VMEM_LIMIT = 48 * 1024 * 1024


def tap_selection():
    select = np.zeros((108, 256), np.float32)
    for first in range(3):
        for second in range(3):
            for third in range(3):
                for chan in range(4):
                    lane = (first % 2 * 64 + third * 16 + chan * 4 + second - 1) % 128
                    row = (9 * first + 3 * second + third) * 4 + chan
                    select[row, first // 2 * 128 + lane] = 1.0
    return select


def dot(left, right, precision=None):
    return jnp.dot(left, right, preferred_element_type=F32, precision=precision)


def dot_lanes(left, right):
    return lax.dot_general(left, right, (((1,), (1,)), ((), ())), preferred_element_type=F32)


def lanes_of(shape):
    return lax.broadcasted_iota(jnp.int32, shape, 1)


def turned(value, shift):
    shift = shift % 128
    return pltpu.roll(value, shift, 1) if shift else value


def from_left(value):
    return jnp.where(lanes_of(value.shape) == 0, 0.0, pltpu.roll(value, 1, 1))


def from_right(value):
    return jnp.where(lanes_of(value.shape) == 127, 0.0, pltpu.roll(value, 127, 1))


def leaky_relu(value):
    return jnp.where(value > 0, value, SLOPE * value)


def slope_mask(value):
    return jnp.where(value > 0, 1.0, SLOPE)


def channel_order():
    row = lax.broadcasted_iota(jnp.int32, (64, 64), 0)
    return jnp.where(lanes_of((64, 64)) == 4 * (row % 16) + row // 16, 1.0, 0.0)


def pack_kernel(
    universe_hbm,
    cotangent_hbm,
    w1_hbm,
    w2_hbm,
    bias1_hbm,
    bias2_hbm,
    owners_hbm,
    accumulated_hbm,
    own_ref,
    late_ref,
    early_ref,
    w1_ref,
    w2_ref,
    bias1_ref,
    bias2_ref,
    owners_ref,
    kept_ref,
    universe_ref,
    cotangent_ref,
    sems,
):
    first = pltpu.make_async_copy(universe_hbm, universe_ref, sems.at[0])
    second = pltpu.make_async_copy(cotangent_hbm, cotangent_ref, sems.at[1])
    first.start()
    second.start()
    pairs = (
        (w1_hbm, w1_ref),
        (w2_hbm, w2_ref),
        (bias1_hbm, bias1_ref),
        (bias2_hbm, bias2_ref),
        (owners_hbm, owners_ref),
        (accumulated_hbm, kept_ref),
    )
    others = [pltpu.make_async_copy(*pair, sems.at[i + 2]) for i, pair in enumerate(pairs)]
    for copy in others:
        copy.start()
    first.wait()
    for deep in range(4):
        rows = jnp.concatenate(
            [universe_ref[0, chan, deep].astype(F32) for chan in range(4)], axis=0
        ).astype(BF16)
        own_ref[deep * 16 : deep * 16 + 16, :] = rows
        if deep > 0:
            late_ref[deep * 16 - 16 : deep * 16, :] = rows
        early_ref[deep * 16 : deep * 16 + 16, :] = rows
    second.wait()
    for group in range(4):
        own_ref[64:80, group * 128 : group * 128 + 128] = cotangent_ref[
            group * 16 : group * 16 + 16, :
        ]
    for copy in others:
        copy.wait()


def weights_kernel(
    rank_ref,
    w1_ref,
    w2_ref,
    bias1_ref,
    bias2_ref,
    owners_ref,
    big1_ref,
    big2_ref,
    back_ref,
    comb_ref,
    wide1_ref,
    wide2_ref,
    target_ref,
    ordered_ref,
):
    for r in range(4):
        cell = lax.broadcasted_iota(jnp.int32, (512, 128), 0)
        comb_ref[:, r * 128 : r * 128 + 128] = jnp.where(
            cell == 4 * lanes_of((512, 128)) + r, 1.0, 0.0
        ).astype(BF16)
    ordered_ref[:, 768:896] = jnp.zeros((64, 128), F32)
    ordered_ref[:, 0:864] = dot(channel_order().astype(BF16), w2_ref[...])
    place = lax.broadcasted_iota(jnp.int32, (32, 32), 0) == lanes_of((32, 32))
    column = jnp.sum(jnp.where(place, bias1_ref[...], 0.0), axis=1, keepdims=True)
    wide1_ref[...] = jnp.broadcast_to(column, (32, 128))
    column = jnp.sum(channel_order() * bias2_ref[...], axis=1, keepdims=True)
    wide2_ref[...] = jnp.broadcast_to(column, (64, 128))

    mine = owners_ref[...] == rank_ref[0]
    member = jnp.broadcast_to(jnp.where(mine, 1.0, 0.0), (8, NB)).astype(BF16)
    earlier = lax.broadcasted_iota(jnp.int32, (NB, NB), 0) < lanes_of((NB, NB))
    before = dot(member, jnp.where(earlier, 1.0, 0.0).astype(BF16))[0:1, :]
    target_ref[:, 384:NB_PAD] = jnp.full((1, 128), -1, jnp.int32)
    target_ref[:, 0:NB] = jnp.where(mine, before.astype(jnp.int32), -1)

    q = lax.broadcasted_iota(jnp.int32, (108, 256), 0)
    tap, chan = q >> 2, q & 3
    first = (tap >= 9).astype(jnp.int32) + (tap >= 18).astype(jnp.int32)
    tap = tap - 9 * first
    second = (tap >= 3).astype(jnp.int32) + (tap >= 6).astype(jnp.int32)
    lane = (first & 1) * 64 + (tap - 3 * second) * 16 + chan * 4 + second - 1
    lane = (first >> 1) * 128 + (lane & 127)
    select = jnp.where(lane == lanes_of((108, 256)), 1.0, 0.0).astype(BF16)
    base = dot(w1_ref[...], select)
    y_of = lanes_of((32, 128)) % 4
    for y in range(4):
        near = jnp.abs(y_of - y) <= 1
        for r in range(2):
            for at in (0, 128):
                part = turned(base[:, at : at + 128], r * 16 + y)
                big1_ref[(y * 2 + r) * 32 : (y * 2 + r) * 32 + 32, at : at + 128] = jnp.where(
                    near, part, 0.0
                ).astype(BF16)
    group = lanes_of((64, 128)) // 32

    def gathered(taps):
        result = jnp.zeros((64, 128), F32)
        for place, tap in enumerate(taps):
            if tap is not None:
                column = ordered_ref[:, tap // 4 * 128 : tap // 4 * 128 + 128]
                result = jnp.where(group == place, turned(column, (place - tap) * 32), result)
        return result

    for first in range(3):
        for second in range(3):
            for ph in range(2):
                taps = [
                    (first * 3 + second) * 3 + col - ph if 0 <= col - ph <= 2 else None
                    for col in range(4)
                ]
                tile = gathered(taps).astype(BF16)
                for y in range(2):
                    other = y + second - 1
                    if 0 <= other < 2:
                        big2_ref[
                            (y * 2 + ph) * 64 : (y * 2 + ph) * 64 + 64,
                            first * 256 + other * 128 : first * 256 + other * 128 + 128,
                        ] = tile
    for first in range(3):
        for other in range(2):
            for pair in range(2):
                tiles = []
                for col in (2 * pair, 2 * pair + 1):
                    taps = [
                        ((2 - first) * 3 + 1 - (other - y)) * 3 + 2 - (col - ph)
                        if 0 <= col - ph <= 2
                        else None
                        for y in range(2)
                        for ph in range(2)
                    ]
                    tiles.append(gathered(taps))
                at = first * 512 + other * 256 + pair * 128
                back_ref[:, at : at + 128] = jnp.concatenate(tiles, axis=0).T.astype(BF16)


def expand(source, comb_ref, field_ref):
    phases = [dot(source, comb_ref[:, r * 128 : r * 128 + 128]) for r in range(4)]
    columns = [from_left(phases[3])] + phases + [from_right(phases[0])]
    for col, part in enumerate(columns):
        part = part.astype(BF16)
        for layer in range(source.shape[0] // 16):
            at = layer * 96 + col * 16
            field_ref[at : at + 16, :] = part[layer * 16 : layer * 16 + 16, :]


def exact_pick(value, select):
    high = value.astype(BF16)
    rest = value - high.astype(F32)
    middle = rest.astype(BF16)
    low = (rest - middle.astype(F32)).astype(BF16)
    rows = value.shape[0]
    moved = dot(jnp.concatenate([high, middle, low], axis=0), select)
    return moved[0:rows] + moved[rows : 2 * rows] + moved[2 * rows : 3 * rows]


def around(layers, half):
    empty = jnp.zeros((64, 128), BF16)
    parts = []
    for deep in range(2):
        for pair in range(2):
            pieces = []
            for first in range(3):
                ref, at = layers(2 * half + deep + first)
                pieces.append(ref[at + pair * 32 : at + pair * 32 + 64, :])
            parts.append(jnp.concatenate(pieces + [empty], axis=0))
    return jnp.concatenate(parts, axis=1)


def stacks(pieces, begin):
    columns = [
        jnp.concatenate([pieces(half) for half in range(at, at + 3)], axis=0)
        for at in (begin, begin + 1)
    ]
    return jnp.concatenate(columns, axis=1)


def pool_first(conv, bias1, pooled_ref, at, pre_ref, pre_at):
    for y in range(2):
        means = []
        for pair in range(2):
            total = None
            for deep in range(2):
                lane = (deep * 2 + pair) * 128
                for row in range(y * 128, y * 128 + 128, 32):
                    block = conv[row : row + 32, lane : lane + 128] + bias1
                    if pre_ref is not None:
                        pre_ref[pre_at + row : pre_at + row + 32, lane : lane + 128] = block
                    value = leaky_relu(block)
                    total = value if total is None else total + value
            means.append((total * 0.125).astype(BF16).astype(F32))
        even, odd = means
        pooled_ref[at + y * 128 : at + y * 128 + 128, :] = jnp.concatenate(
            [from_left(odd), even, odd, from_right(even)], axis=0
        ).astype(BF16)


def delta_second(conv, bias2, cotangent_ref, delta2_ref):
    plain = [cotangent_ref[64:80, g * 128 : g * 128 + 128] for g in range(4)]
    upstream = dot(channel_order().astype(BF16), jnp.concatenate(plain, axis=0)) * 0.125
    total = jnp.zeros((64, 128), F32)
    for half in range(2):
        lane = half * 128
        for y in range(2):
            deltas = []
            for ph in range(2):
                row = (y * 2 + ph) * 64
                block = conv[row : row + 64, lane : lane + 128] + bias2
                total = total + leaky_relu(block)
                deltas.append((upstream * slope_mask(block)).astype(BF16).astype(F32))
            at = half * 512 + y * 256
            delta2_ref[at : at + 256, :] = jnp.concatenate(
                [from_left(deltas[1]), deltas[0], deltas[1], from_right(deltas[0])], axis=0
            ).astype(BF16)
    return total


def late_kernel(
    own_ref,
    next_ref,
    after_ref,
    big1_ref,
    big2_ref,
    comb_ref,
    wide1_ref,
    wide2_ref,
    field_ref,
    pooled_ref,
    pre_ref,
    delta2_ref,
):
    source = jnp.concatenate(
        [own_ref[0:64, :], next_ref[0:64, :], after_ref[0:48, :]], axis=0
    )
    expand(source, comb_ref, field_ref)

    def layers(layer):
        return field_ref, (layer - 3) * 96

    for half in range(2, 6):
        conv = dot(big1_ref[...], around(layers, half))
        kept = pre_ref if half < 4 else None
        pool_first(conv, wide1_ref[...], pooled_ref, (half - 2) * 256, kept, (half - 2) * 256)

    def pooled(half):
        return pooled_ref[(half - 2) * 256 : (half - 1) * 256, :]

    conv = dot(big2_ref[...], stacks(pooled, 2))
    delta_second(conv, wide2_ref[...], next_ref, delta2_ref)


def main_kernel(
    prev_ref,
    own_ref,
    late_field_ref,
    late_pooled_ref,
    pre_ref,
    late_delta2_ref,
    big1_ref,
    big2_ref,
    back_ref,
    comb_ref,
    wide1_ref,
    wide2_ref,
    select_ref,
    feature_ref,
    blocks_ref,
    field_ref,
    pooled_ref,
    delta2_ref,
    delta1_ref,
    order_ref,
):
    expand(prev_ref[...], comb_ref, field_ref)

    def layers(layer):
        return (field_ref, layer * 96) if layer < 3 else (late_field_ref, (layer - 3) * 96)

    def pooled(half):
        ref, at = (pooled_ref, half * 256) if half < 2 else (late_pooled_ref, (half - 2) * 256)
        return ref[at : at + 256, :]

    def delta_rows(half, begin, rows):
        ref, at = (delta2_ref, half * 512) if half < 2 else (late_delta2_ref, (half - 2) * 512)
        return ref[at + begin : at + begin + rows, :]

    for half in range(2):
        conv = dot(big1_ref[...], around(layers, half))
        pool_first(conv, wide1_ref[...], pooled_ref, half * 256, None, 0)
    conv = dot(big2_ref[...], stacks(pooled, 0))
    feature = delta_second(conv, wide2_ref[...], own_ref, delta2_ref) * 0.125
    for u in range(4):
        order_ref[pl.ds(u, 16, stride=4), :] = feature[u * 16 : u * 16 + 16, :]
    feature_ref[...] = order_ref[...].astype(BF16)

    ones = jnp.ones((8, 256), BF16)
    delta = jnp.concatenate(
        [
            jnp.concatenate([delta_rows(half, y * 256 + 64, 128) for half in (1, 2)], axis=1)
            for y in range(2)
        ],
        axis=0,
    )
    grad2 = dot_lanes(delta, stacks(pooled, 1))
    bias_sum2 = dot_lanes(ones, delta)

    backs = dot(back_ref[...], stacks(lambda half: delta_rows(half, 0, 512), 0)) * 0.125
    ones = jnp.ones((8, 512), BF16)
    grad1 = None
    bias_sum1 = None
    for half in range(2):
        for deep in range(2):
            for pair in range(2):
                lane = (deep * 2 + pair) * 128
                for row in range(0, 256, 32):
                    slot = (row // 128 * 2 + pair) * 32
                    back = backs[slot : slot + 32, half * 128 : half * 128 + 128]
                    at = half * 256 + row
                    delta1_ref[at : at + 32, lane : lane + 128] = (
                        back * slope_mask(pre_ref[at : at + 32, lane : lane + 128])
                    ).astype(BF16)
        delta = delta1_ref[half * 256 : half * 256 + 256, :]
        term = dot_lanes(delta, around(layers, half + 2))
        bias_term = dot_lanes(ones, delta)
        grad1 = term if grad1 is None else grad1 + term
        bias_sum1 = bias_term if bias_sum1 is None else bias_sum1 + bias_term

    exact = lax.Precision.HIGHEST
    bias_row1 = bias_sum1[:, 0:128] + bias_sum1[:, 128:256]
    bias_row1 = bias_row1 + turned(bias_row1, 64)
    bias_row1 = bias_row1 + turned(bias_row1, 32)
    q = lax.broadcasted_iota(jnp.int32, (128, 128), 0)
    lane = 32 + 4 * (q % 16) + q % 64 // 16
    bias_row2 = dot(
        bias_sum2[:, 0:128] + bias_sum2[:, 128:256],
        jnp.where(lane == lanes_of((128, 128)), 1.0, 0.0),
        exact,
    )

    y_of = lanes_of((32, 128)) % 4
    parts = []
    for at in (0, 128):
        part = jnp.zeros((32, 128), F32)
        for y in range(4):
            near = jnp.abs(y_of - y) <= 1
            for r in range(2):
                row = (y * 2 + r) * 32
                block = grad1[row : row + 32, at : at + 128]
                part = part + turned(jnp.where(near, block, 0.0), -(r * 16 + y))
        parts.append(part)
    flat1 = dot(jnp.concatenate(parts, axis=1), select_ref[...], exact)
    rows = [None] * 28
    lane8 = lanes_of((8, 128))
    for o in range(32):
        begin = o * 108 // 128
        shift = o * 108 % 128
        moved = turned(flat1[o // 8 * 8 : o // 8 * 8 + 8, :], shift)
        for row, kept in ((begin, lane8 >= shift), (begin + 1, lane8 < shift)):
            if row == begin or shift + 108 > 128:
                term = jnp.where(kept, moved, 0.0)[o % 8 : o % 8 + 1, :]
                rows[row] = term if rows[row] is None else rows[row] + term
    for row in range(27):
        blocks_ref[row : row + 1, :] = rows[row]

    taps = []
    for first in range(3):
        for second in range(3):
            part = None
            for y in range(2):
                other = y + second - 1
                if 0 <= other < 2:
                    for ph in range(2):
                        row = (y * 2 + ph) * 64
                        at = first * 256 + other * 128
                        block = turned(grad2[row : row + 64, at : at + 128], -ph * 32)
                        part = block if part is None else part + block
            taps.append(part)
    group = lanes_of((16, 128)) // 32

    def chunk(number, place):
        u, tap = (number - 1) // 27, (number - 1) % 27
        return turned(taps[tap // 3][u * 16 : u * 16 + 16, :], (place - tap % 3) * 32)

    last = pltpu.roll(chunk(108, 0), 1, 0)
    row_of = lax.broadcasted_iota(jnp.int32, (16, 128), 0)
    for k in range(27):
        if k == 0:
            value = jnp.where(row_of == 0, jnp.broadcast_to(bias_row1[0:1, :], (16, 128)), last)
        else:
            value = chunk(4 * k, 0)
        for place in range(1, 4):
            value = jnp.where(group == place, chunk(4 * k + place, place), value)
        blocks_ref[pl.ds(27 + k, 16, stride=27), :] = value
    blocks_ref[459:460, :] = jnp.where(lanes_of((1, 128)) < 32, last[0:1, :], bias_row2[0:1, :])
    blocks_ref[NB:NB_PAD, :] = jnp.zeros((NB_PAD - NB, 128), F32)


def owned_kernel(blocks_ref, target_ref, kept_ref, feature_ref, feature_out_ref, owned_ref):
    feature_out_ref[...] = feature_ref[...]
    capacity = owned_ref.shape[0]
    rows = -(-capacity // 16) * 16
    blocks = blocks_ref[...]
    high = blocks.astype(BF16)
    rest = blocks - high.astype(F32)
    middle = rest.astype(BF16)
    low = (rest - middle.astype(F32)).astype(BF16)
    row_at = lax.broadcasted_iota(jnp.int32, (rows, NB_PAD), 0)
    placing = jnp.where(row_at == target_ref[...], 1.0, 0.0).astype(BF16)
    moved = dot(placing, jnp.concatenate([high, middle, low], axis=1))
    total = moved[:, 0:128] + moved[:, 128:256] + moved[:, 256:384]
    owned_ref[...] = kept_ref[...] + total[0:capacity, :]


def whole():
    return pl.BlockSpec(memory_space=pltpu.VMEM)


def params():
    return pltpu.CompilerParams(vmem_limit_bytes=VMEM_LIMIT)


def pack(*operands):
    universe, cotangent, *others = operands
    return pl.pallas_call(
        pack_kernel,
        out_shape=(
            jax.ShapeDtypeStruct((80, 512), BF16),
            jax.ShapeDtypeStruct((48, 512), BF16),
            jax.ShapeDtypeStruct((64, 512), BF16),
            *(jax.ShapeDtypeStruct(x.shape, x.dtype) for x in others),
        ),
        in_specs=[pl.BlockSpec(memory_space=pltpu.HBM)] * 8,
        out_specs=(whole(),) * 9,
        scratch_shapes=[
            pltpu.VMEM(universe.shape, BF16),
            pltpu.VMEM(cotangent.shape, BF16),
            pltpu.SemaphoreType.DMA((8,)),
        ],
        compiler_params=params(),
        cost_estimate=pl.CostEstimate(flops=1 << 16, bytes_accessed=1 << 18, transcendentals=0),
    )(*(pltpu.with_memory_space_constraint(x, pltpu.HBM) for x in operands))


def expand_weights(rank, *operands):
    return pl.pallas_call(
        weights_kernel,
        out_shape=(
            jax.ShapeDtypeStruct((256, 256), BF16),
            jax.ShapeDtypeStruct((256, 768), BF16),
            jax.ShapeDtypeStruct((128, 1536), BF16),
            jax.ShapeDtypeStruct((512, 512), BF16),
            jax.ShapeDtypeStruct((32, 128), F32),
            jax.ShapeDtypeStruct((64, 128), F32),
            jax.ShapeDtypeStruct((1, NB_PAD), jnp.int32),
        ),
        in_specs=[pl.BlockSpec(memory_space=pltpu.SMEM)] + [whole()] * 5,
        out_specs=(whole(),) * 7,
        scratch_shapes=[pltpu.VMEM((64, 896), F32)],
        compiler_params=params(),
        cost_estimate=pl.CostEstimate(flops=1 << 26, bytes_accessed=4 << 20, transcendentals=0),
    )(rank, *operands)


def forward_late(own, following, after, big1, big2, comb, wide1, wide2):
    return pl.pallas_call(
        late_kernel,
        out_shape=(
            jax.ShapeDtypeStruct((11 * 96, 128), BF16),
            jax.ShapeDtypeStruct((4 * 256, 128), BF16),
            jax.ShapeDtypeStruct((2 * 256, 512), F32),
            jax.ShapeDtypeStruct((2 * 512, 128), BF16),
        ),
        in_specs=[whole()] * 8,
        out_specs=(whole(),) * 4,
        compiler_params=params(),
        cost_estimate=pl.CostEstimate(flops=1 << 30, bytes_accessed=4 << 20, transcendentals=0),
    )(own, following, after, big1, big2, comb, wide1, wide2)


def forward_backward(before, own, late, weights):
    return pl.pallas_call(
        main_kernel,
        out_shape=(
            jax.ShapeDtypeStruct((64, 128), BF16),
            jax.ShapeDtypeStruct((NB_PAD, 128), F32),
        ),
        in_specs=[whole()] * 13,
        out_specs=(whole(),) * 2,
        scratch_shapes=[
            pltpu.VMEM((3 * 96, 128), BF16),
            pltpu.VMEM((2 * 256, 128), BF16),
            pltpu.VMEM((2 * 512, 128), BF16),
            pltpu.VMEM((2 * 256, 512), BF16),
            pltpu.VMEM((64, 128), F32),
        ],
        compiler_params=params(),
        cost_estimate=pl.CostEstimate(flops=1 << 30, bytes_accessed=4 << 20, transcendentals=0),
    )(before, own, *late, *weights, jnp.asarray(np.pad(tap_selection().T, ((0, 0), (0, 20))), F32))


def add_owned(blocks, target, kept, feature):
    return pl.pallas_call(
        owned_kernel,
        out_shape=(
            jax.ShapeDtypeStruct(feature.shape, feature.dtype),
            jax.ShapeDtypeStruct(kept.shape, kept.dtype),
        ),
        in_specs=[whole()] * 4,
        out_specs=(whole(),) * 2,
        compiler_params=params(),
        cost_estimate=pl.CostEstimate(flops=1 << 27, bytes_accessed=1 << 20, transcendentals=0),
    )(blocks, target, kept, feature)


SLAB = ("z_hi", "y", "core")
DP = ("z_lo", "x")
PLANE = ("x", "z_lo", "z_hi")
REST = ("core", "y")


def exchange(rows, axes):
    return lax.all_to_all(rows, axes, 0, 0, tiled=True)


def sum_everywhere(blocks):
    width = blocks.shape[1]
    plane, rest = lax.axis_size(PLANE), lax.axis_size(REST)
    part = exchange(blocks, PLANE).reshape(plane, -1, width).sum(axis=0)
    part = exchange(jnp.tile(part, (rest, 1)), REST).reshape(rest, -1, width).sum(axis=0)
    return exchange(jnp.tile(part, (plane, 1)), PLANE)


def body(
    universe, cotangent, conv1_weight, conv1_bias, conv2_weight, conv2_bias, owners, accumulated
):
    slabs = lax.axis_size(SLAB)
    packed, late, early, *others, kept = pack(
        universe,
        cotangent.reshape(64, 128),
        conv1_weight,
        conv2_weight,
        conv1_bias.reshape(1, 32),
        conv2_bias.reshape(1, 64),
        owners.reshape(1, NB),
        accumulated,
    )
    def from_slab(distance, rows):
        pairs = [(i, (i - distance) % slabs) for i in range(slabs)]
        return lax.ppermute(rows, SLAB, pairs)

    before, following, after = from_slab(-1, late), from_slab(1, packed), from_slab(2, early)
    *weights, target = expand_weights(lax.axis_index(DP).reshape(1), *others)
    big1, big2, _, comb, wide1, wide2 = weights
    ahead = forward_late(packed, following, after, big1, big2, comb, wide1, wide2)
    feature, blocks = forward_backward(before, packed, ahead, weights)
    feature, owned = add_owned(sum_everywhere(blocks), target, kept, feature)
    return (feature.reshape(1, 64, 1, 1, 128), owned)


def split_mesh(mesh):
    slabs, ranks = mesh.devices.shape
    x = min(4, ranks)
    y = min(8, slabs // 2)
    shape = (slabs // (2 * y), y, 2, ranks // x, x)
    return Mesh(mesh.devices.reshape(shape), SLAB + DP)


def solution(mesh):
    in_specs = (
        P(DP, None, SLAB, None, None),
        P(DP, None, SLAB, None, None),
        P(),
        P(),
        P(),
        P(),
        P(),
        P(DP, None),
    )
    out_specs = (P(DP, None, SLAB, None, None), P(DP, None))
    return jax.shard_map(
        body, mesh=split_mesh(mesh), in_specs=in_specs, out_specs=out_specs, check_vma=False
    )
```

```python
import jax
import jax.numpy as jnp
import numpy as np
from jax import lax
from jax.experimental import pallas as pl
from jax.experimental.pallas import tpu as pltpu
from jax.sharding import Mesh
from jax.sharding import PartitionSpec as P

NB = 460
NB_PAD = 512
SLOPE = 0.3
BF16 = jnp.bfloat16
F32 = jnp.float32
VMEM_LIMIT = 48 * 1024 * 1024


def tap_selection():
    select = np.zeros((108, 256), np.float32)
    for first in range(3):
        for second in range(3):
            for third in range(3):
                for chan in range(4):
                    lane = (first % 2 * 64 + third * 16 + chan * 4 + second - 1) % 128
                    row = (9 * first + 3 * second + third) * 4 + chan
                    select[row, first // 2 * 128 + lane] = 1.0
    return select


def dot(left, right, precision=None):
    return jnp.dot(left, right, preferred_element_type=F32, precision=precision)


def dot_lanes(left, right):
    return lax.dot_general(left, right, (((1,), (1,)), ((), ())), preferred_element_type=F32)


def lanes_of(shape):
    return lax.broadcasted_iota(jnp.int32, shape, 1)


def turned(value, shift):
    shift = shift % 128
    return pltpu.roll(value, shift, 1) if shift else value


def from_left(value):
    return jnp.where(lanes_of(value.shape) == 0, 0.0, pltpu.roll(value, 1, 1))


def from_right(value):
    return jnp.where(lanes_of(value.shape) == 127, 0.0, pltpu.roll(value, 127, 1))


def leaky_relu(value):
    return jnp.where(value > 0, value, SLOPE * value)


def slope_mask(value):
    return jnp.where(value > 0, 1.0, SLOPE)


def channel_order():
    row = lax.broadcasted_iota(jnp.int32, (64, 64), 0)
    return jnp.where(lanes_of((64, 64)) == 4 * (row % 16) + row // 16, 1.0, 0.0)


def pack_kernel(
    universe_hbm,
    cotangent_hbm,
    w1_hbm,
    w2_hbm,
    bias1_hbm,
    bias2_hbm,
    owners_hbm,
    accumulated_hbm,
    own_ref,
    late_ref,
    early_ref,
    w1_ref,
    w2_ref,
    bias1_ref,
    bias2_ref,
    owners_ref,
    kept_ref,
    universe_ref,
    cotangent_ref,
    sems,
):
    first = pltpu.make_async_copy(universe_hbm, universe_ref, sems.at[0])
    second = pltpu.make_async_copy(cotangent_hbm, cotangent_ref, sems.at[1])
    first.start()
    second.start()
    pairs = (
        (w1_hbm, w1_ref),
        (w2_hbm, w2_ref),
        (bias1_hbm, bias1_ref),
        (bias2_hbm, bias2_ref),
        (owners_hbm, owners_ref),
        (accumulated_hbm, kept_ref),
    )
    others = [pltpu.make_async_copy(*pair, sems.at[i + 2]) for i, pair in enumerate(pairs)]
    for copy in others:
        copy.start()
    first.wait()
    for deep in range(4):
        rows = jnp.concatenate(
            [universe_ref[0, chan, deep].astype(F32) for chan in range(4)], axis=0
        ).astype(BF16)
        own_ref[deep * 16 : deep * 16 + 16, :] = rows
        if deep > 0:
            late_ref[deep * 16 - 16 : deep * 16, :] = rows
        early_ref[deep * 16 : deep * 16 + 16, :] = rows
    second.wait()
    for group in range(4):
        own_ref[64:80, group * 128 : group * 128 + 128] = cotangent_ref[
            group * 16 : group * 16 + 16, :
        ]
    for copy in others:
        copy.wait()


def weights_kernel(
    rank_ref,
    w1_ref,
    w2_ref,
    bias1_ref,
    bias2_ref,
    owners_ref,
    big1_ref,
    big2_ref,
    back_ref,
    comb_ref,
    wide1_ref,
    wide2_ref,
    target_ref,
    ordered_ref,
):
    for r in range(4):
        cell = lax.broadcasted_iota(jnp.int32, (512, 128), 0)
        comb_ref[:, r * 128 : r * 128 + 128] = jnp.where(
            cell == 4 * lanes_of((512, 128)) + r, 1.0, 0.0
        ).astype(BF16)
    ordered_ref[:, 768:896] = jnp.zeros((64, 128), F32)
    ordered_ref[:, 0:864] = dot(channel_order().astype(BF16), w2_ref[...])
    place = lax.broadcasted_iota(jnp.int32, (32, 32), 0) == lanes_of((32, 32))
    column = jnp.sum(jnp.where(place, bias1_ref[...], 0.0), axis=1, keepdims=True)
    wide1_ref[...] = jnp.broadcast_to(column, (32, 128))
    column = jnp.sum(channel_order() * bias2_ref[...], axis=1, keepdims=True)
    wide2_ref[...] = jnp.broadcast_to(column, (64, 128))

    mine = owners_ref[...] == rank_ref[0]
    member = jnp.broadcast_to(jnp.where(mine, 1.0, 0.0), (8, NB)).astype(BF16)
    earlier = lax.broadcasted_iota(jnp.int32, (NB, NB), 0) < lanes_of((NB, NB))
    before = dot(member, jnp.where(earlier, 1.0, 0.0).astype(BF16))[0:1, :]
    target_ref[:, 384:NB_PAD] = jnp.full((1, 128), -1, jnp.int32)
    target_ref[:, 0:NB] = jnp.where(mine, before.astype(jnp.int32), -1)

    q = lax.broadcasted_iota(jnp.int32, (108, 256), 0)
    tap, chan = q >> 2, q & 3
    first = (tap >= 9).astype(jnp.int32) + (tap >= 18).astype(jnp.int32)
    tap = tap - 9 * first
    second = (tap >= 3).astype(jnp.int32) + (tap >= 6).astype(jnp.int32)
    lane = (first & 1) * 64 + (tap - 3 * second) * 16 + chan * 4 + second - 1
    lane = (first >> 1) * 128 + (lane & 127)
    select = jnp.where(lane == lanes_of((108, 256)), 1.0, 0.0).astype(BF16)
    base = dot(w1_ref[...], select)
    y_of = lanes_of((32, 128)) % 4
    for y in range(4):
        near = jnp.abs(y_of - y) <= 1
        for r in range(2):
            for at in (0, 128):
                part = turned(base[:, at : at + 128], r * 16 + y)
                big1_ref[(y * 2 + r) * 32 : (y * 2 + r) * 32 + 32, at : at + 128] = jnp.where(
                    near, part, 0.0
                ).astype(BF16)
    group = lanes_of((64, 128)) // 32

    def gathered(taps):
        result = jnp.zeros((64, 128), F32)
        for place, tap in enumerate(taps):
            if tap is not None:
                column = ordered_ref[:, tap // 4 * 128 : tap // 4 * 128 + 128]
                result = jnp.where(group == place, turned(column, (place - tap) * 32), result)
        return result

    for first in range(3):
        for second in range(3):
            for ph in range(2):
                taps = [
                    (first * 3 + second) * 3 + col - ph if 0 <= col - ph <= 2 else None
                    for col in range(4)
                ]
                tile = gathered(taps).astype(BF16)
                for y in range(2):
                    other = y + second - 1
                    if 0 <= other < 2:
                        big2_ref[
                            (y * 2 + ph) * 64 : (y * 2 + ph) * 64 + 64,
                            first * 256 + other * 128 : first * 256 + other * 128 + 128,
                        ] = tile
    for first in range(3):
        for other in range(2):
            for pair in range(2):
                tiles = []
                for col in (2 * pair, 2 * pair + 1):
                    taps = [
                        ((2 - first) * 3 + 1 - (other - y)) * 3 + 2 - (col - ph)
                        if 0 <= col - ph <= 2
                        else None
                        for y in range(2)
                        for ph in range(2)
                    ]
                    tiles.append(gathered(taps))
                at = first * 512 + other * 256 + pair * 128
                back_ref[:, at : at + 128] = jnp.concatenate(tiles, axis=0).T.astype(BF16)


def expand(source, comb_ref, field_ref):
    phases = [dot(source, comb_ref[:, r * 128 : r * 128 + 128]) for r in range(4)]
    columns = [from_left(phases[3])] + phases + [from_right(phases[0])]
    for col, part in enumerate(columns):
        part = part.astype(BF16)
        for layer in range(source.shape[0] // 16):
            at = layer * 96 + col * 16
            field_ref[at : at + 16, :] = part[layer * 16 : layer * 16 + 16, :]


def exact_pick(value, select):
    high = value.astype(BF16)
    rest = value - high.astype(F32)
    middle = rest.astype(BF16)
    low = (rest - middle.astype(F32)).astype(BF16)
    rows = value.shape[0]
    moved = dot(jnp.concatenate([high, middle, low], axis=0), select)
    return moved[0:rows] + moved[rows : 2 * rows] + moved[2 * rows : 3 * rows]


def around(layers, half):
    empty = jnp.zeros((64, 128), BF16)
    parts = []
    for deep in range(2):
        for pair in range(2):
            pieces = []
            for first in range(3):
                ref, at = layers(2 * half + deep + first)
                pieces.append(ref[at + pair * 32 : at + pair * 32 + 64, :])
            parts.append(jnp.concatenate(pieces + [empty], axis=0))
    return jnp.concatenate(parts, axis=1)


def stacks(pieces, begin):
    columns = [
        jnp.concatenate([pieces(half) for half in range(at, at + 3)], axis=0)
        for at in (begin, begin + 1)
    ]
    return jnp.concatenate(columns, axis=1)


def pool_first(conv, bias1, pooled_ref, at, pre_ref, pre_at):
    for y in range(2):
        means = []
        for pair in range(2):
            total = None
            for deep in range(2):
                lane = (deep * 2 + pair) * 128
                for row in range(y * 128, y * 128 + 128, 32):
                    block = conv[row : row + 32, lane : lane + 128] + bias1
                    if pre_ref is not None:
                        pre_ref[pre_at + row : pre_at + row + 32, lane : lane + 128] = block
                    value = leaky_relu(block)
                    total = value if total is None else total + value
            means.append((total * 0.125).astype(BF16).astype(F32))
        even, odd = means
        pooled_ref[at + y * 128 : at + y * 128 + 128, :] = jnp.concatenate(
            [from_left(odd), even, odd, from_right(even)], axis=0
        ).astype(BF16)


def delta_second(conv, bias2, cotangent_ref, delta2_ref):
    plain = [cotangent_ref[64:80, g * 128 : g * 128 + 128] for g in range(4)]
    upstream = dot(channel_order().astype(BF16), jnp.concatenate(plain, axis=0)) * 0.125
    total = jnp.zeros((64, 128), F32)
    for half in range(2):
        lane = half * 128
        for y in range(2):
            deltas = []
            for ph in range(2):
                row = (y * 2 + ph) * 64
                block = conv[row : row + 64, lane : lane + 128] + bias2
                total = total + leaky_relu(block)
                deltas.append((upstream * slope_mask(block)).astype(BF16).astype(F32))
            at = half * 512 + y * 256
            delta2_ref[at : at + 256, :] = jnp.concatenate(
                [from_left(deltas[1]), deltas[0], deltas[1], from_right(deltas[0])], axis=0
            ).astype(BF16)
    return total


def late_kernel(
    own_ref,
    next_ref,
    after_ref,
    big1_ref,
    big2_ref,
    comb_ref,
    wide1_ref,
    wide2_ref,
    field_ref,
    pooled_ref,
    pre_ref,
    delta2_ref,
):
    source = jnp.concatenate(
        [own_ref[0:64, :], next_ref[0:64, :], after_ref[0:48, :]], axis=0
    )
    expand(source, comb_ref, field_ref)

    def layers(layer):
        return field_ref, (layer - 3) * 96

    for half in range(2, 6):
        conv = dot(big1_ref[...], around(layers, half))
        kept = pre_ref if half < 4 else None
        pool_first(conv, wide1_ref[...], pooled_ref, (half - 2) * 256, kept, (half - 2) * 256)

    def pooled(half):
        return pooled_ref[(half - 2) * 256 : (half - 1) * 256, :]

    conv = dot(big2_ref[...], stacks(pooled, 2))
    delta_second(conv, wide2_ref[...], next_ref, delta2_ref)


def main_kernel(
    prev_ref,
    own_ref,
    late_field_ref,
    late_pooled_ref,
    pre_ref,
    late_delta2_ref,
    big1_ref,
    big2_ref,
    back_ref,
    comb_ref,
    wide1_ref,
    wide2_ref,
    select_ref,
    feature_ref,
    blocks_ref,
    field_ref,
    pooled_ref,
    delta2_ref,
    delta1_ref,
    order_ref,
):
    expand(prev_ref[...], comb_ref, field_ref)

    def layers(layer):
        return (field_ref, layer * 96) if layer < 3 else (late_field_ref, (layer - 3) * 96)

    def pooled(half):
        ref, at = (pooled_ref, half * 256) if half < 2 else (late_pooled_ref, (half - 2) * 256)
        return ref[at : at + 256, :]

    def delta_rows(half, begin, rows):
        ref, at = (delta2_ref, half * 512) if half < 2 else (late_delta2_ref, (half - 2) * 512)
        return ref[at + begin : at + begin + rows, :]

    for half in range(2):
        conv = dot(big1_ref[...], around(layers, half))
        pool_first(conv, wide1_ref[...], pooled_ref, half * 256, None, 0)
    conv = dot(big2_ref[...], stacks(pooled, 0))
    feature = delta_second(conv, wide2_ref[...], own_ref, delta2_ref) * 0.125
    for u in range(4):
        order_ref[pl.ds(u, 16, stride=4), :] = feature[u * 16 : u * 16 + 16, :]
    feature_ref[...] = order_ref[...].astype(BF16)

    ones = jnp.ones((8, 256), BF16)
    delta = jnp.concatenate(
        [
            jnp.concatenate([delta_rows(half, y * 256 + 64, 128) for half in (1, 2)], axis=1)
            for y in range(2)
        ],
        axis=0,
    )
    grad2 = dot_lanes(delta, stacks(pooled, 1))
    bias_sum2 = dot_lanes(ones, delta)

    backs = dot(back_ref[...], stacks(lambda half: delta_rows(half, 0, 512), 0)) * 0.125
    ones = jnp.ones((8, 512), BF16)
    grad1 = None
    bias_sum1 = None
    for half in range(2):
        for deep in range(2):
            for pair in range(2):
                lane = (deep * 2 + pair) * 128
                for row in range(0, 256, 32):
                    slot = (row // 128 * 2 + pair) * 32
                    back = backs[slot : slot + 32, half * 128 : half * 128 + 128]
                    at = half * 256 + row
                    delta1_ref[at : at + 32, lane : lane + 128] = (
                        back * slope_mask(pre_ref[at : at + 32, lane : lane + 128])
                    ).astype(BF16)
        delta = delta1_ref[half * 256 : half * 256 + 256, :]
        term = dot_lanes(delta, around(layers, half + 2))
        bias_term = dot_lanes(ones, delta)
        grad1 = term if grad1 is None else grad1 + term
        bias_sum1 = bias_term if bias_sum1 is None else bias_sum1 + bias_term

    bias_row1 = bias_sum1[:, 0:128] + bias_sum1[:, 128:256]
    bias_row1 = bias_row1 + turned(bias_row1, 64)
    bias_row1 = bias_row1 + turned(bias_row1, 32)
    q = lax.broadcasted_iota(jnp.int32, (128, 128), 0)
    lane = 32 + 4 * (q % 16) + q % 64 // 16
    both = jnp.concatenate([bias_sum2[:, 0:128] + bias_sum2[:, 128:256]] * 2, axis=0)
    order = jnp.where(lane == lanes_of((128, 128)), 1.0, 0.0).astype(BF16)
    bias_row2 = exact_pick(both, order)

    y_of = lanes_of((32, 128)) % 4
    parts = []
    for at in (0, 128):
        part = jnp.zeros((32, 128), F32)
        for y in range(4):
            near = jnp.abs(y_of - y) <= 1
            for r in range(2):
                row = (y * 2 + r) * 32
                block = grad1[row : row + 32, at : at + 128]
                part = part + turned(jnp.where(near, block, 0.0), -(r * 16 + y))
        parts.append(part)
    flat1 = exact_pick(jnp.concatenate(parts, axis=1), select_ref[...])
    rows = [None] * 28
    lane8 = lanes_of((8, 128))
    for o in range(32):
        begin = o * 108 // 128
        shift = o * 108 % 128
        moved = turned(flat1[o // 8 * 8 : o // 8 * 8 + 8, :], shift)
        for row, kept in ((begin, lane8 >= shift), (begin + 1, lane8 < shift)):
            if row == begin or shift + 108 > 128:
                term = jnp.where(kept, moved, 0.0)[o % 8 : o % 8 + 1, :]
                rows[row] = term if rows[row] is None else rows[row] + term
    for row in range(27):
        blocks_ref[row : row + 1, :] = rows[row]

    taps = []
    for first in range(3):
        for second in range(3):
            part = None
            for y in range(2):
                other = y + second - 1
                if 0 <= other < 2:
                    for ph in range(2):
                        row = (y * 2 + ph) * 64
                        at = first * 256 + other * 128
                        block = turned(grad2[row : row + 64, at : at + 128], -ph * 32)
                        part = block if part is None else part + block
            taps.append(part)
    group = lanes_of((16, 128)) // 32

    def chunk(number, place):
        u, tap = (number - 1) // 27, (number - 1) % 27
        return turned(taps[tap // 3][u * 16 : u * 16 + 16, :], (place - tap % 3) * 32)

    last = pltpu.roll(chunk(108, 0), 1, 0)
    row_of = lax.broadcasted_iota(jnp.int32, (16, 128), 0)
    for k in range(27):
        if k == 0:
            value = jnp.where(row_of == 0, jnp.broadcast_to(bias_row1[0:1, :], (16, 128)), last)
        else:
            value = chunk(4 * k, 0)
        for place in range(1, 4):
            value = jnp.where(group == place, chunk(4 * k + place, place), value)
        blocks_ref[pl.ds(27 + k, 16, stride=27), :] = value
    blocks_ref[459:460, :] = jnp.where(lanes_of((1, 128)) < 32, last[0:1, :], bias_row2[0:1, :])
    blocks_ref[NB:NB_PAD, :] = jnp.zeros((NB_PAD - NB, 128), F32)


def owned_kernel(blocks_ref, target_ref, kept_ref, feature_ref, feature_out_ref, owned_ref):
    feature_out_ref[...] = feature_ref[...]
    capacity = owned_ref.shape[0]
    rows = -(-capacity // 16) * 16
    blocks = blocks_ref[...]
    high = blocks.astype(BF16)
    rest = blocks - high.astype(F32)
    middle = rest.astype(BF16)
    low = (rest - middle.astype(F32)).astype(BF16)
    row_at = lax.broadcasted_iota(jnp.int32, (rows, NB_PAD), 0)
    placing = jnp.where(row_at == target_ref[...], 1.0, 0.0).astype(BF16)
    moved = dot(placing, jnp.concatenate([high, middle, low], axis=1))
    total = moved[:, 0:128] + moved[:, 128:256] + moved[:, 256:384]
    owned_ref[...] = kept_ref[...] + total[0:capacity, :]


def whole():
    return pl.BlockSpec(memory_space=pltpu.VMEM)


def params():
    return pltpu.CompilerParams(vmem_limit_bytes=VMEM_LIMIT)


def pack(*operands):
    universe, cotangent, *others = operands
    return pl.pallas_call(
        pack_kernel,
        out_shape=(
            jax.ShapeDtypeStruct((80, 512), BF16),
            jax.ShapeDtypeStruct((48, 512), BF16),
            jax.ShapeDtypeStruct((64, 512), BF16),
            *(jax.ShapeDtypeStruct(x.shape, x.dtype) for x in others),
        ),
        in_specs=[pl.BlockSpec(memory_space=pltpu.HBM)] * 8,
        out_specs=(whole(),) * 9,
        scratch_shapes=[
            pltpu.VMEM(universe.shape, BF16),
            pltpu.VMEM(cotangent.shape, BF16),
            pltpu.SemaphoreType.DMA((8,)),
        ],
        compiler_params=params(),
        cost_estimate=pl.CostEstimate(flops=1 << 16, bytes_accessed=1 << 18, transcendentals=0),
    )(*(pltpu.with_memory_space_constraint(x, pltpu.HBM) for x in operands))


def expand_weights(rank, *operands):
    return pl.pallas_call(
        weights_kernel,
        out_shape=(
            jax.ShapeDtypeStruct((256, 256), BF16),
            jax.ShapeDtypeStruct((256, 768), BF16),
            jax.ShapeDtypeStruct((128, 1536), BF16),
            jax.ShapeDtypeStruct((512, 512), BF16),
            jax.ShapeDtypeStruct((32, 128), F32),
            jax.ShapeDtypeStruct((64, 128), F32),
            jax.ShapeDtypeStruct((1, NB_PAD), jnp.int32),
        ),
        in_specs=[pl.BlockSpec(memory_space=pltpu.SMEM)] + [whole()] * 5,
        out_specs=(whole(),) * 7,
        scratch_shapes=[pltpu.VMEM((64, 896), F32)],
        compiler_params=params(),
        cost_estimate=pl.CostEstimate(flops=1 << 26, bytes_accessed=4 << 20, transcendentals=0),
    )(rank, *operands)


def forward_late(own, following, after, big1, big2, comb, wide1, wide2):
    return pl.pallas_call(
        late_kernel,
        out_shape=(
            jax.ShapeDtypeStruct((11 * 96, 128), BF16),
            jax.ShapeDtypeStruct((4 * 256, 128), BF16),
            jax.ShapeDtypeStruct((2 * 256, 512), F32),
            jax.ShapeDtypeStruct((2 * 512, 128), BF16),
        ),
        in_specs=[whole()] * 8,
        out_specs=(whole(),) * 4,
        compiler_params=params(),
        cost_estimate=pl.CostEstimate(flops=1 << 30, bytes_accessed=4 << 20, transcendentals=0),
    )(own, following, after, big1, big2, comb, wide1, wide2)


def forward_backward(before, own, late, weights):
    return pl.pallas_call(
        main_kernel,
        out_shape=(
            jax.ShapeDtypeStruct((64, 128), BF16),
            jax.ShapeDtypeStruct((NB_PAD, 128), F32),
        ),
        in_specs=[whole()] * 13,
        out_specs=(whole(),) * 2,
        scratch_shapes=[
            pltpu.VMEM((3 * 96, 128), BF16),
            pltpu.VMEM((2 * 256, 128), BF16),
            pltpu.VMEM((2 * 512, 128), BF16),
            pltpu.VMEM((2 * 256, 512), BF16),
            pltpu.VMEM((64, 128), F32),
        ],
        compiler_params=params(),
        cost_estimate=pl.CostEstimate(flops=1 << 30, bytes_accessed=4 << 20, transcendentals=0),
    )(before, own, *late, *weights, jnp.asarray(np.pad(tap_selection().T, ((0, 0), (0, 20))), BF16))


def add_owned(blocks, target, kept, feature):
    return pl.pallas_call(
        owned_kernel,
        out_shape=(
            jax.ShapeDtypeStruct(feature.shape, feature.dtype),
            jax.ShapeDtypeStruct(kept.shape, kept.dtype),
        ),
        in_specs=[whole()] * 4,
        out_specs=(whole(),) * 2,
        compiler_params=params(),
        cost_estimate=pl.CostEstimate(flops=1 << 27, bytes_accessed=1 << 20, transcendentals=0),
    )(blocks, target, kept, feature)


SLAB = ("z_hi", "y", "core")
DP = ("z_lo", "x")
PLANE = ("x", "z_lo", "z_hi")
REST = ("core", "y")


def exchange(rows, axes):
    return lax.all_to_all(rows, axes, 0, 0, tiled=True)


def sum_everywhere(blocks):
    width = blocks.shape[1]
    plane, rest = lax.axis_size(PLANE), lax.axis_size(REST)
    part = exchange(blocks, PLANE).reshape(plane, -1, width).sum(axis=0)
    part = exchange(jnp.tile(part, (rest, 1)), REST).reshape(rest, -1, width).sum(axis=0)
    return exchange(jnp.tile(part, (plane, 1)), PLANE)


def body(
    universe, cotangent, conv1_weight, conv1_bias, conv2_weight, conv2_bias, owners, accumulated
):
    slabs = lax.axis_size(SLAB)
    packed, late, early, *others, kept = pack(
        universe,
        cotangent.reshape(64, 128),
        conv1_weight,
        conv2_weight,
        conv1_bias.reshape(1, 32),
        conv2_bias.reshape(1, 64),
        owners.reshape(1, NB),
        accumulated,
    )
    def from_slab(distance, rows):
        pairs = [(i, (i - distance) % slabs) for i in range(slabs)]
        return lax.ppermute(rows, SLAB, pairs)

    before, following, after = from_slab(-1, late), from_slab(1, packed), from_slab(2, early)
    *weights, target = expand_weights(lax.axis_index(DP).reshape(1), *others)
    big1, big2, _, comb, wide1, wide2 = weights
    ahead = forward_late(packed, following, after, big1, big2, comb, wide1, wide2)
    feature, blocks = forward_backward(before, packed, ahead, weights)
    feature, owned = add_owned(sum_everywhere(blocks), target, kept, feature)
    return (feature.reshape(1, 64, 1, 1, 128), owned)


def split_mesh(mesh):
    slabs, ranks = mesh.devices.shape
    x = min(4, ranks)
    y = min(8, slabs // 2)
    shape = (slabs // (2 * y), y, 2, ranks // x, x)
    return Mesh(mesh.devices.reshape(shape), SLAB + DP)


def solution(mesh):
    in_specs = (
        P(DP, None, SLAB, None, None),
        P(DP, None, SLAB, None, None),
        P(),
        P(),
        P(),
        P(),
        P(),
        P(DP, None),
    )
    out_specs = (P(DP, None, SLAB, None, None), P(DP, None))
    return jax.shard_map(
        body, mesh=split_mesh(mesh), in_specs=in_specs, out_specs=out_specs, check_vma=False
    )
```
